32 devices in a mesh: dp: 8 (over z, x), mp: 4 (over y, core).
Axes of the slice: x: 2, y: 2, z: 4, core: 2. Of those that a mesh axis runs over, the one named last changes fastest.
Arguments:
- latent: bfloat16 [16, 256, 1280], P('dp', 'mp'), may hold values from -30 to 30
- text_embeds: bfloat16 [16, 77, 2048], P('dp'), may hold values from -6 to 6
- cotangent: bfloat16 [16, 256, 1280], P('dp', 'mp'), may hold values from -11 to 11
- item_count: int32 [8], P('dp'), may hold values from 1 to 2, as said below
- bucket: int32 [16], P('dp'), may hold values from 0 to 2
- timestep: int32 [16], P('dp'), may hold values from 0 to 999
- conv_in: bfloat16 [3, 3, 1280, 1280], P(None, None, 'dp', 'mp'), may hold values from -0.0546875 to 0.0546875
- conv_out: bfloat16 [3, 3, 1280, 1280], P(None, None, 'mp', 'dp'), may hold values from -0.078125 to 0.078125
- time_weight: bfloat16 [1280, 1280], P('dp', 'mp'), may hold values from -0.15625 to 0.15625
- self_query: bfloat16 [1280, 1280], P('dp', 'mp'), may hold values from -0.15625 to 0.15625
- self_key: bfloat16 [1280, 1280], P('dp', 'mp'), may hold values from -0.15625 to 0.15625
- self_value: bfloat16 [1280, 1280], P('dp', 'mp'), may hold values from -0.15625 to 0.15625
- self_out: bfloat16 [1280, 1280], P('mp', 'dp'), may hold values from -1.25 to 1.25
- cross_query: bfloat16 [1280, 1280], P('dp', 'mp'), may hold values from -0.15625 to 0.15625
- cross_key: bfloat16 [2048, 1280], P('dp', 'mp'), may hold values from -0.125 to 0.125
- cross_value: bfloat16 [2048, 1280], P('dp', 'mp'), may hold values from -0.125 to 0.125
- cross_out: bfloat16 [1280, 1280], P('mp', 'dp'), may hold values from -0.75 to 0.75
- ff_value: bfloat16 [1280, 5120], P('dp', 'mp'), may hold values from -0.15625 to 0.15625
- ff_gate: bfloat16 [1280, 5120], P('dp', 'mp'), may hold values from -0.15625 to 0.15625
- ff_down: bfloat16 [5120, 1280], P('mp', 'dp'), may hold values from -0.125 to 0.125
- gn_in_gain: bfloat16 [1280], P('dp'), may hold values from 0.099609375 to 1.8984375
- gn_mid_gain: bfloat16 [1280], P('dp'), may hold values from 0.099609375 to 1.8984375
- self_gain: bfloat16 [1280], P('dp'), may hold values from 0.099609375 to 1.8984375
- cross_gain: bfloat16 [1280], P('dp'), may hold values from 0.099609375 to 1.8984375
- ff_gain: bfloat16 [1280], P('dp'), may hold values from 0.099609375 to 1.8984375
Outputs:
- output: bfloat16 [16, 256, 1280], P('dp', 'mp')
- latent_grad: bfloat16 [16, 256, 1280], P('dp', 'mp')
- conv_in_grad: float32 [3, 3, 1280, 1280], P(None, None, 'dp', 'mp')
- conv_out_grad: float32 [3, 3, 1280, 1280], P(None, None, 'mp', 'dp')
- time_weight_grad: float32 [1280, 1280], P('dp', 'mp')
- self_query_grad: float32 [1280, 1280], P('dp', 'mp')
- self_key_grad: float32 [1280, 1280], P('dp', 'mp')
- self_value_grad: float32 [1280, 1280], P('dp', 'mp')
- self_out_grad: float32 [1280, 1280], P('mp', 'dp')
- cross_query_grad: float32 [1280, 1280], P('dp', 'mp')
- cross_key_grad: float32 [2048, 1280], P('dp', 'mp')
- cross_value_grad: float32 [2048, 1280], P('dp', 'mp')
- cross_out_grad: float32 [1280, 1280], P('mp', 'dp')
- ff_value_grad: float32 [1280, 5120], P('dp', 'mp')
- ff_gate_grad: float32 [1280, 5120], P('dp', 'mp')
- ff_down_grad: float32 [5120, 1280], P('mp', 'dp')
- gn_in_gain_grad: float32 [1280], P('dp')
- gn_mid_gain_grad: float32 [1280], P('dp')
- self_gain_grad: float32 [1280], P('dp')
- cross_gain_grad: float32 [1280], P('dp')
- ff_gain_grad: float32 [1280], P('dp')
The draws below stay inside these ranges and needn't reach their ends.
Inputs may be any that keep to these rules, and one draw needn't show every extreme that they name: `item_count`: A data group's items stand in its first slots; one group holds 2 items and another one item.
All inputs are finite; a program needn't handle non-finite values.
Results may differ from the reference program's by a relative error of at most 0.025.
Values may be sent and summed in bfloat16 or wider, within the bound.
No kernel may reach another device: no remote copies, remote signals or barrier semaphores. Data moves between devices by JAX's collectives and lax.ppermute only.
A program may use at most 384 MiB of HBM per device.

```python
import math
import jax
import jax.numpy as jnp
from jax import lax

C = 1280
HEAD_DIM = 64
CTX = 2048
TEXT = 77
GN_GROUPS = 32
FF = 5120
SIDE = 16
SLOTS = 2
ROWS = 256
GROUPS = 8
ITEMS = 16


def rising_rows():
    position = jnp.arange(ROWS, dtype=jnp.float32) / ROWS
    return jnp.exp(math.log(3.0) * (position - 0.5))


def draw_latent(key, part):
    key = jax.random.fold_in(key, 11)
    base_key, channel_key = jax.random.split(key, 2)
    row_scale = rising_rows()
    channel_scale = jnp.exp(jax.random.uniform(channel_key, (C,), jnp.float32, math.log(0.4), math.log(2.5)))
    base_values = jnp.clip(jax.random.normal(base_key, (ITEMS, ROWS, C), jnp.float32), -6.0, 6.0)
    return (base_values * row_scale[None, :, None] * channel_scale[None, None, :]).astype(jnp.bfloat16)


def draw_cotangent(key, part):
    key = jax.random.fold_in(key, 17)
    base_key = jax.random.fold_in(key, 0)
    row_scale = rising_rows()
    base_values = jnp.clip(jax.random.normal(base_key, (ITEMS, ROWS, C), jnp.float32), -6.0, 6.0)
    return (base_values * row_scale[None, :, None]).astype(jnp.bfloat16)


def draw_item_count(key, part):
    key = jax.random.fold_in(key, 5)
    count_key, ranking_key = jax.random.split(key)
    counts = jax.random.randint(count_key, (GROUPS,), 1, SLOTS + 1)
    ranking = jax.random.permutation(ranking_key, GROUPS)
    group_number = jnp.arange(GROUPS, dtype=jnp.int32)
    counts = jnp.where(group_number == ranking[0], SLOTS, counts)
    counts = jnp.where(group_number == ranking[1], 1, counts)
    return counts.astype(jnp.int32)


def plant(values, own_key, smallest, largest):
    shape = values.shape
    spot = [jax.random.randint(jax.random.fold_in(own_key, axis), (), 0, shape[axis]) for axis in range(len(shape))]
    values = values.at[tuple(spot)].set(smallest)
    longest = shape.index(max(shape))
    spot[longest] = (spot[longest] + 1) % shape[longest]
    return values.at[tuple(spot)].set(largest)


def level_of(key, extent, cuts, least, largest):
    def one(dim, shards_of):
        steps = jax.random.uniform(jax.random.fold_in(jax.random.fold_in(key, 6), dim), (shards_of,), jnp.float32, least / len(cuts), largest / len(cuts))
        return jnp.repeat(jnp.exp(steps), extent[dim] // shards_of).reshape((-1,) + (1,) * (len(extent) - dim - 1))

    loudness = one(*cuts[0])
    for cut in cuts[1:]:
        loudness = loudness * one(*cut)
    return loudness


def scatter_about(stream_key, shape, deviation, most, cuts=(), kind=jnp.bfloat16):
    drawn = jax.random.normal(stream_key, shape, jnp.float32) * deviation
    if len(cuts) > 0:
        drawn = level_of(stream_key, shape, cuts, -0.22, 0.18) * drawn
    return jnp.clip(drawn, min=-most, max=most).astype(kind)


def setup_inputs(seed: int = 0) -> dict:
    keys = jax.random.split(jax.random.key(seed), 26)
    latent = draw_latent(jax.random.fold_in(keys[25], 71), 0)
    text_embeds = scatter_about(keys[1], (ITEMS, TEXT, CTX), 1.0, 6.0, ((0, 8),))
    cotangent = draw_cotangent(jax.random.fold_in(keys[25], 71), 0)
    item_count = draw_item_count(jax.random.fold_in(keys[25], 71), 0)
    bucket = plant(jax.random.randint(keys[4], (ITEMS,), 0, 3), jax.random.fold_in(keys[4], 1), 0, 2).astype(jnp.int32)
    timestep = plant(jax.random.randint(keys[5], (ITEMS,), 0, 1000), jax.random.fold_in(keys[5], 1), 0, 999).astype(jnp.int32)
    conv_in = scatter_about(keys[6], (3, 3, C, C), (9 * C) ** -0.5, 0.0546875, ((2, 8), (3, 4)))
    conv_out = scatter_about(keys[7], (3, 3, C, C), (9 * C // 2) ** -0.5, 0.078125, ((2, 4), (3, 8)))
    time_weight = scatter_about(keys[8], (C, C), C ** -0.5, 0.15625, ((0, 8), (1, 4)))
    self_query = scatter_about(keys[9], (C, C), C ** -0.5, 0.15625, ((0, 8), (1, 4)))
    self_key = scatter_about(keys[10], (C, C), C ** -0.5, 0.15625, ((0, 8), (1, 4)))
    self_value = scatter_about(keys[11], (C, C), C ** -0.5, 0.15625, ((0, 8), (1, 4)))
    self_out = scatter_about(keys[12], (C, C), (max(4 * C // ROWS, 1)) ** -0.5, 1.25, ((0, 4), (1, 8)))
    cross_query = scatter_about(keys[13], (C, C), C ** -0.5, 0.15625, ((0, 8), (1, 4)))
    cross_key = scatter_about(keys[14], (CTX, C), CTX ** -0.5, 0.125, ((0, 8), (1, 4)))
    cross_value = scatter_about(keys[15], (CTX, C), CTX ** -0.5, 0.125, ((0, 8), (1, 4)))
    cross_out = scatter_about(keys[16], (C, C), (max(4 * C // TEXT, 1)) ** -0.5, 0.75, ((0, 4), (1, 8)))
    ff_value = scatter_about(keys[17], (C, FF), C ** -0.5, 0.15625, ((0, 8), (1, 4)))
    ff_gate = scatter_about(keys[18], (C, FF), C ** -0.5, 0.15625, ((0, 8), (1, 4)))
    ff_down = scatter_about(keys[19], (FF, C), (FF // 2) ** -0.5, 0.125, ((0, 4), (1, 8)))
    gn_in_gain = jnp.clip(1.0 + 0.18 * jax.random.normal(keys[20], (C,), jnp.float32), 0.099609375, 1.8984375).astype(jnp.bfloat16)
    gn_mid_gain = jnp.clip(1.0 + 0.18 * jax.random.normal(keys[21], (C,), jnp.float32), 0.099609375, 1.8984375).astype(jnp.bfloat16)
    self_gain = jnp.clip(1.0 + 0.18 * jax.random.normal(keys[22], (C,), jnp.float32), 0.099609375, 1.8984375).astype(jnp.bfloat16)
    cross_gain = jnp.clip(1.0 + 0.18 * jax.random.normal(keys[23], (C,), jnp.float32), 0.099609375, 1.8984375).astype(jnp.bfloat16)
    ff_gain = jnp.clip(1.0 + 0.18 * jax.random.normal(keys[24], (C,), jnp.float32), 0.099609375, 1.8984375).astype(jnp.bfloat16)
    return dict(latent=latent, text_embeds=text_embeds, cotangent=cotangent, item_count=item_count, bucket=bucket, timestep=timestep, conv_in=conv_in, conv_out=conv_out, time_weight=time_weight, self_query=self_query, self_key=self_key, self_value=self_value, self_out=self_out, cross_query=cross_query, cross_key=cross_key, cross_value=cross_value, cross_out=cross_out, ff_value=ff_value, ff_gate=ff_gate, ff_down=ff_down, gn_in_gain=gn_in_gain, gn_mid_gain=gn_mid_gain, self_gain=self_gain, cross_gain=cross_gain, ff_gain=ff_gain)


@jax.custom_vjp
def low(v):
    return lax.optimization_barrier(v.astype(jnp.bfloat16)).astype(jnp.float32)

@jax.custom_vjp
def low_back(v):
    return v

def low_keep(v):
    return (low(v), None)

def low_pass(kept, grad):
    return (grad,)

def back_keep(v):
    return (v, None)

def back_low(kept, grad):
    return (low(grad),)
low.defvjp(low_keep, low_pass)
low_back.defvjp(back_keep, back_low)
highest = lax.Precision.HIGHEST

def both_ways(values):
    return low_back(low(values))

def matmul(former, latter):
    return jnp.dot(former, latter, precision=highest, preferred_element_type=jnp.float32)

def layer_norm(hidden, factor):
    center = hidden - lax.optimization_barrier(jnp.mean(hidden, axis=-1, keepdims=True))
    spread = lax.optimization_barrier(jnp.mean(center * center, axis=-1, keepdims=True))
    return center * lax.rsqrt(spread + 1e-05) * factor

def group_norm(values, row_mask, counts):
    grouped = values.reshape(ROWS, GN_GROUPS, C // GN_GROUPS)
    average = lax.optimization_barrier(jnp.sum(grouped, axis=(0, 2))) / counts
    center = (grouped - average[None, :, None]) * row_mask[:, None, None]
    variance = lax.optimization_barrier(jnp.sum(center * center, axis=(0, 2))) / counts
    standard = (grouped - average[None, :, None]) * lax.rsqrt(variance + 1e-06)[None, :, None]
    return standard.reshape(ROWS, C)

def step_embedding(steps):
    half_width = C // 2
    frequencies = jnp.exp(-math.log(10000.0) * jnp.arange(half_width, dtype=jnp.float32) / half_width)
    angles = steps.astype(jnp.float32)[:, None] * frequencies[None, :]
    return jnp.concatenate([jnp.cos(angles), jnp.sin(angles)], axis=1)

def convolve(values, kernel, item_width):
    border = 2 * SIDE
    padded = jnp.pad(values, ((border, border), (0, 0)))
    column = jnp.arange(ROWS, dtype=jnp.int32) % item_width
    summed = jnp.zeros((ROWS, kernel.shape[3]), jnp.float32)
    for row_step in range(3):
        for column_step in range(3):
            shift_start = border + (row_step - 1) * item_width + (column_step - 1)
            source = lax.dynamic_slice_in_dim(padded, shift_start, ROWS, 0)
            usable = (column + column_step - 1 >= 0) & (column + column_step - 1 < item_width)
            summed = summed + matmul(jnp.where(usable[:, None], source, 0.0), kernel[row_step, column_step])
    return summed

def attention(query_rows, key_rows, value_rows, key_valid):
    heads_here = query_rows.shape[1] // HEAD_DIM
    query_heads = query_rows.reshape(query_rows.shape[0], heads_here, HEAD_DIM)
    key_heads = key_rows.reshape(key_rows.shape[0], heads_here, HEAD_DIM)
    value_heads = value_rows.reshape(value_rows.shape[0], heads_here, HEAD_DIM)
    scores = jnp.einsum('qhd,khd->hqk', query_heads, key_heads, precision=highest) * HEAD_DIM ** (-0.5)
    scores = jnp.where(key_valid[None, None, :], low_back(scores), -1e+30)
    shares = low(jax.nn.softmax(scores, axis=-1))
    mixture = jnp.einsum('hqk,khd->qhd', shares, value_heads, precision=highest)
    return both_ways(mixture.reshape(query_rows.shape[0], heads_here * HEAD_DIM))

def item_block(params, member):
    latent_rows, text_rows, row_mask, key_valid, counts, item_width, time_act = member
    conv_in, conv_out, time_weight, self_query, self_key, self_value, self_out, cross_query, cross_key, cross_value, cross_out, ff_value, ff_gate, ff_down, gn_in_gain, gn_mid_gain, self_gain, cross_gain, ff_gain = params
    keep_rows = row_mask[:, None]
    masked = latent_rows * keep_rows
    first_act = low(jax.nn.silu(group_norm(masked, row_mask, counts) * gn_in_gain) * keep_rows)
    time_added = matmul(time_act[None, :], time_weight)
    middle = low_back((convolve(first_act, conv_in, item_width) + time_added) * keep_rows)
    second_act = low(jax.nn.silu(group_norm(middle, row_mask, counts) * gn_mid_gain) * keep_rows)
    resnet = (masked + low_back(convolve(second_act, conv_out, item_width))) * keep_rows
    attend_in = low(layer_norm(resnet, self_gain))
    mixture = attention(both_ways(matmul(attend_in, self_query)), both_ways(matmul(attend_in, self_key)), both_ways(matmul(attend_in, self_value)), key_valid)
    after_self = resnet + low_back(matmul(mixture, self_out))
    cross_in = low(layer_norm(after_self, cross_gain))
    every_token = jnp.ones((text_rows.shape[0],), dtype=jnp.bool_)
    cross_mix = attention(both_ways(matmul(cross_in, cross_query)), both_ways(matmul(text_rows, cross_key)), both_ways(matmul(text_rows, cross_value)), every_token)
    after_cross = after_self + low_back(matmul(cross_mix, cross_out))
    feed_in = low(layer_norm(after_cross, ff_gain))
    value_part = low_back(matmul(feed_in, ff_value))
    gate_part = low_back(matmul(feed_in, ff_gate))
    hidden = low(value_part * jax.nn.gelu(gate_part, approximate=False))
    return (after_cross + low_back(matmul(hidden, ff_down))) * keep_rows

def reference(latent, text_embeds, cotangent, item_count, bucket, timestep, conv_in, conv_out, time_weight, self_query, self_key, self_value, self_out, cross_query, cross_key, cross_value, cross_out, ff_value, ff_gate, ff_down, gn_in_gain, gn_mid_gain, self_gain, cross_gain, ff_gain):
    params = (conv_in.astype(jnp.float32), conv_out.astype(jnp.float32), time_weight.astype(jnp.float32), self_query.astype(jnp.float32), self_key.astype(jnp.float32), self_value.astype(jnp.float32), self_out.astype(jnp.float32), cross_query.astype(jnp.float32), cross_key.astype(jnp.float32), cross_value.astype(jnp.float32), cross_out.astype(jnp.float32), ff_value.astype(jnp.float32), ff_gate.astype(jnp.float32), ff_down.astype(jnp.float32), gn_in_gain.astype(jnp.float32), gn_mid_gain.astype(jnp.float32), self_gain.astype(jnp.float32), cross_gain.astype(jnp.float32), ff_gain.astype(jnp.float32))
    slot_index = jnp.arange(ITEMS, dtype=jnp.int32) % SLOTS
    group_index = jnp.arange(ITEMS, dtype=jnp.int32) // SLOTS
    is_live = (slot_index < jnp.take(item_count, group_index)).astype(jnp.float32)
    widths = jnp.where(bucket == 0, SIDE, jnp.where(bucket == 1, 5 * SIDE // 4, 3 * SIDE // 2)).astype(jnp.int32)
    heights = jnp.where(bucket == 0, SIDE, jnp.where(bucket == 1, 3 * SIDE // 4, 5 * SIDE // 8)).astype(jnp.int32)
    filled = widths * heights
    position = jnp.arange(ROWS, dtype=jnp.int32)
    inside = position[None, :] < filled[:, None]
    row_mask = inside.astype(jnp.float32) * is_live[:, None]
    counts = filled.astype(jnp.float32) * (C // GN_GROUPS)
    text_rows = text_embeds.astype(jnp.float32)
    time_act = low(jax.nn.silu(step_embedding(timestep)))

    def regroup(values):
        return values.reshape((GROUPS, SLOTS) + values.shape[1:])
    members = (regroup(text_rows), regroup(row_mask), regroup(inside), regroup(counts), regroup(widths), regroup(time_act))

    def forward(latent_rows, weights):

        def one_item(single):
            return item_block(weights, single)

        def one_group(member):
            return jax.vmap(one_item)(member)
        result = lax.map(jax.checkpoint(one_group), (regroup(latent_rows),) + members)
        return result.reshape(ITEMS, ROWS, C)
    output, pullback = jax.vjp(forward, latent.astype(jnp.float32), params)
    latent_grad, gradients = pullback(cotangent.astype(jnp.float32))
    return (output.astype(jnp.bfloat16), latent_grad.astype(jnp.bfloat16), gradients[0], gradients[1], gradients[2], gradients[3], gradients[4], gradients[5], gradients[6], gradients[7], gradients[8], gradients[9], gradients[10], gradients[11], gradients[12], gradients[13], gradients[14], gradients[15], gradients[16], gradients[17], gradients[18])
```

```python
import math

import jax
import jax.numpy as jnp
from jax import lax
from jax.sharding import PartitionSpec as P

C = 1280
HEAD_DIM = 64
GN_GROUPS = 32
SIDE = 16
TAPS = 9

highest = lax.Precision.HIGHEST
f32 = jnp.float32
bf16 = jnp.bfloat16


def ring_order(size):
    return list(range(0, size, 2)) + list(range(size - 1, 0, -2))


def ring_pairs(size):
    order = ring_order(size)
    right = [(order[i], order[(i + 1) % size]) for i in range(size)]
    return right, [(b, a) for a, b in right]


def ring_place(size):
    order = ring_order(size)
    place = jnp.array([order.index(i) for i in range(size)], jnp.int32)
    return jnp.array(order, jnp.int32), place[lax.axis_index("dp")]


def ring_gather(block):
    size = lax.axis_size("dp")
    rows, columns = block.shape
    if size != 8:
        return lax.all_gather(block, "dp", axis=0, tiled=True)
    right, left = ring_pairs(size)
    order, place = ring_place(size)
    half = rows // 2
    zero = jnp.int32(0)

    def put(whole, part, away, start):
        owner = order[(place + away) % size]
        return lax.dynamic_update_slice(whole, part[None], (owner, jnp.int32(start), zero))

    whole = put(jnp.zeros((size, rows, columns), block.dtype), block, 0, 0)
    from_left = from_right = block
    for step in range(1, size // 2):
        from_left = lax.ppermute(from_left, "dp", right)
        from_right = lax.ppermute(from_right, "dp", left)
        whole = put(whole, from_left, size - step, 0)
        whole = put(whole, from_right, step, 0)
    from_left = lax.ppermute(from_left[:half], "dp", right)
    from_right = lax.ppermute(from_right[half:], "dp", left)
    whole = put(whole, from_left, size // 2, 0)
    whole = put(whole, from_right, size // 2, half)
    return whole.reshape(size * rows, columns)


def ring_scatter(grad):
    size = lax.axis_size("dp")
    rows, columns = grad.shape[0] // size, grad.shape[1]
    if size != 8:
        return lax.psum_scatter(grad, "dp", scatter_dimension=0, tiled=True).astype(f32)
    right, left = ring_pairs(size)
    order, place = ring_place(size)
    half = rows // 2
    blocks = grad.reshape(size, rows, columns)

    def own(away):
        return lax.dynamic_index_in_dim(blocks, order[(place + away) % size], 0, keepdims=False)

    far = own(size // 2)
    to_right = lax.ppermute(far[:half], "dp", right)
    to_left = lax.ppermute(far[half:], "dp", left)
    for step in range(size // 2 - 1, 0, -1):
        ahead, behind = own(step), own(size - step)
        if step == size // 2 - 1:
            ahead = jnp.concatenate([ahead[:half].astype(f32) + to_right, ahead[half:].astype(f32)])
            behind = jnp.concatenate([behind[:half].astype(f32), behind[half:].astype(f32) + to_left])
        else:
            ahead = ahead.astype(f32) + to_right
            behind = behind.astype(f32) + to_left
        to_right = lax.ppermute(ahead.astype(bf16), "dp", right)
        to_left = lax.ppermute(behind.astype(bf16), "dp", left)
    return own(0).astype(f32) + to_right.astype(f32) + to_left.astype(f32)


def share_small(values, axis):
    size = lax.axis_size(axis)
    return lax.all_to_all(
        jnp.broadcast_to(values[None], (size,) + values.shape), axis, 0, 0, tiled=True
    )


def mp_bits():
    me = lax.axis_index("mp")
    return me % 2, me // 2


NEAR = [(0, 1), (1, 0), (2, 3), (3, 2)]
FAR = [(0, 2), (2, 0), (1, 3), (3, 1)]


def gather_rows(values):
    near_bit, far_bit = mp_bits()
    far = lax.ppermute(values, "mp", FAR)
    near = lax.ppermute(values, "mp", NEAR)
    both = lax.ppermute(far, "mp", NEAR)

    def pair(mine, other, bit):
        return jnp.concatenate(
            [jnp.where(bit == 0, mine, other), jnp.where(bit == 0, other, mine)], axis=1
        )

    return pair(pair(values, near, near_bit), pair(far, both, near_bit), far_bit)


def sum_rows(values):
    near_bit, far_bit = mp_bits()
    items, rows, columns = values.shape
    parts = values.reshape(items, 2, 2, rows // 4, columns)

    def near_part(bit):
        return lax.dynamic_index_in_dim(parts, bit, 2, keepdims=False)

    got = lax.ppermute(near_part(1 - near_bit).astype(bf16), "mp", NEAR)
    held = near_part(near_bit).astype(f32) + got.astype(f32)

    def far_part(bit):
        return lax.dynamic_index_in_dim(held, bit, 1, keepdims=False)

    got = lax.ppermute(far_part(1 - far_bit).astype(bf16), "mp", FAR)
    return far_part(far_bit) + got.astype(f32)


def product(former, latter):
    return jnp.einsum("sna,ab->snb", former, latter, preferred_element_type=f32)


def product_back(former, latter):
    return jnp.einsum("snb,ab->sna", former, latter, preferred_element_type=f32)


def weight_grad(former, latter):
    return jnp.einsum("sna,snb->ab", former, latter, preferred_element_type=f32).astype(bf16)


def tap_matrices(widths, item_rows):
    row = jnp.arange(item_rows, dtype=jnp.int32)
    step = jnp.arange(TAPS, dtype=jnp.int32)
    row_step, column_step = step // 3 - 1, step % 3 - 1
    column = row[None, :] % widths[:, None]
    beside = column[:, None, :] + column_step[None, :, None]
    usable = (beside >= 0) & (beside < widths[:, None, None])
    source = (
        row[None, None, :]
        + row_step[None, :, None] * widths[:, None, None]
        + column_step[None, :, None]
    )
    source = jnp.where(usable, source, -1)
    return (source[:, :, :, None] == row[None, None, None, :]).astype(bf16)


def shift_stack(taps, values):
    stacked = jnp.einsum("strq,sqi->srti", taps, values, preferred_element_type=f32)
    return stacked.astype(bf16).reshape(values.shape[:2] + (TAPS * values.shape[2],))


def shift_stack_back(taps, values):
    stacked = jnp.einsum("strq,sro->sqto", taps, values, preferred_element_type=f32)
    return stacked.astype(bf16).reshape(values.shape[:2] + (TAPS * values.shape[2],))


def shift_sum(taps, values):
    parts = values.astype(bf16).reshape(values.shape[:2] + (TAPS, values.shape[2] // TAPS))
    return jnp.einsum("strq,sqto->sro", taps, parts, preferred_element_type=f32)


def shift_sum_back(taps, values):
    parts = values.astype(bf16).reshape(values.shape[:2] + (TAPS, values.shape[2] // TAPS))
    return jnp.einsum("strq,srti->sqi", taps, parts, preferred_element_type=f32)


def norm_rows(hidden, factor):
    center = hidden - jnp.mean(hidden, axis=-1, keepdims=True)
    scaling = lax.rsqrt(jnp.mean(center * center, axis=-1, keepdims=True) + 1e-05)
    normal = center * scaling
    return ((normal * factor).astype(bf16), normal, scaling)


def norm_rows_back(gradient, normal, scaling, factor):
    scaled = gradient * factor
    offset = jnp.mean(scaled, axis=-1, keepdims=True)
    slopes = jnp.mean(scaled * normal, axis=-1, keepdims=True)
    return (scaling * (scaled - offset - normal * slopes), jnp.sum(gradient * normal, axis=(0, 1)))


def group_sum(values, per_group):
    rows_summed = jnp.sum(values, axis=1)
    return rows_summed.reshape(values.shape[0], values.shape[2] // per_group, per_group).sum(-1)


def spread(values, per_group):
    return jnp.repeat(values, per_group, axis=-1)[:, None, :]


def silu_back(scaled, gradient):
    share = jax.nn.sigmoid(scaled)
    return gradient * share * (1.0 + scaled * (1.0 - share))


def split_heads(values):
    return values.reshape(values.shape[0], values.shape[1], values.shape[2] // HEAD_DIM, HEAD_DIM)


def attend(query_rows, key_rows, value_rows, key_valid):
    scores = jnp.einsum(
        "sqhd,skhd->shqk",
        split_heads(query_rows),
        split_heads(key_rows),
        preferred_element_type=f32,
    ) * HEAD_DIM ** (-0.5)
    if key_valid is not None:
        scores = jnp.where(key_valid[:, None, None, :], scores, -1e30)
    exponent = jnp.exp(scores - jnp.max(scores, axis=-1, keepdims=True))
    chances = exponent / jnp.sum(exponent, axis=-1, keepdims=True)
    mixture = jnp.einsum(
        "shqk,skhd->sqhd",
        chances.astype(bf16),
        split_heads(value_rows),
        preferred_element_type=f32,
    )
    return mixture.reshape(query_rows.shape).astype(bf16), chances


def attend_back(query_rows, key_rows, value_rows, mixture_grad, chances):
    query_heads = split_heads(query_rows)
    key_heads = split_heads(key_rows)
    value_heads = split_heads(value_rows)
    grad_heads = split_heads(mixture_grad)
    value_grad = jnp.einsum(
        "shqk,sqhd->skhd", chances.astype(bf16), grad_heads, preferred_element_type=f32
    )
    share_grad = jnp.einsum(
        "sqhd,skhd->shqk", grad_heads, value_heads, preferred_element_type=f32
    )
    inner_sum = jnp.sum(chances * share_grad, axis=-1, keepdims=True)
    score_grad = (chances * (share_grad - inner_sum)).astype(bf16)
    query_grad = jnp.einsum(
        "shqk,skhd->sqhd", score_grad, key_heads, preferred_element_type=f32
    ) * HEAD_DIM ** (-0.5)
    key_grad = jnp.einsum(
        "shqk,sqhd->skhd", score_grad, query_heads, preferred_element_type=f32
    ) * HEAD_DIM ** (-0.5)
    return (
        query_grad.reshape(query_rows.shape).astype(bf16),
        key_grad.reshape(key_rows.shape).astype(bf16),
        value_grad.reshape(value_rows.shape).astype(bf16),
    )


def body(
    latent,
    text_embeds,
    cotangent,
    item_count,
    bucket,
    timestep,
    conv_in,
    conv_out,
    time_weight,
    self_query,
    self_key,
    self_value,
    self_out,
    cross_query,
    cross_key,
    cross_value,
    cross_out,
    ff_value,
    ff_gate,
    ff_down,
    gn_in_gain,
    gn_mid_gain,
    self_gain,
    cross_gain,
    ff_gain,
):
    slot_count, local_rows, channels = latent.shape
    dp_size, mp_size = lax.axis_size("dp"), lax.axis_size("mp")
    item_rows = local_rows * mp_size
    per_group = channels // GN_GROUPS
    own_channels = conv_in.shape[3]
    share = conv_in.shape[2]
    dp_index, mp_index = lax.axis_index("dp"), lax.axis_index("mp")
    is_live = (jnp.arange(slot_count, dtype=jnp.int32) < item_count[0]).astype(f32)
    widths = jnp.where(
        bucket == 0, SIDE, jnp.where(bucket == 1, 5 * SIDE // 4, 3 * SIDE // 2)
    ).astype(jnp.int32)
    heights = jnp.where(
        bucket == 0, SIDE, jnp.where(bucket == 1, 3 * SIDE // 4, 5 * SIDE // 8)
    ).astype(jnp.int32)
    filled = widths * heights
    position = mp_index * local_rows + jnp.arange(local_rows, dtype=jnp.int32)
    row_mask = (position[None, :] < filled[:, None]).astype(f32) * is_live[:, None]
    key_valid = jnp.arange(item_rows, dtype=jnp.int32)[None, :] < filled[:, None]
    full_mask = key_valid.astype(f32) * is_live[:, None]
    keep = row_mask[:, :, None]
    keep_all = full_mask[:, :, None]
    counts = filled.astype(f32) * per_group
    channel_start = mp_index * own_channels
    taps = tap_matrices(widths, item_rows)

    gain_parts = jnp.stack([gn_in_gain, gn_mid_gain, self_gain, cross_gain, ff_gain]).astype(f32)
    small = jnp.concatenate([gain_parts.reshape(-1), timestep.astype(f32)])
    small_all = share_small(small, "dp")
    gains = small_all[:, : 5 * share].reshape(dp_size, 5, share)
    gains = jnp.swapaxes(gains, 0, 1).reshape(5, channels)
    gain_in_f, gain_self_f, gain_cross_f, gain_feed_f = gains[0], gains[2], gains[3], gains[4]
    gain_mid_own = lax.dynamic_slice_in_dim(gains[1], channel_start, own_channels)
    steps_all = small_all[:, 5 * share :].reshape(-1)

    w_in = ring_gather(
        jnp.swapaxes(conv_in.reshape(TAPS, share, own_channels), 0, 1).reshape(share, -1)
    )
    w_out = ring_gather(
        jnp.transpose(conv_out.reshape(TAPS, own_channels, share), (2, 0, 1)).reshape(share, -1)
    )
    w_self = ring_gather(
        jnp.concatenate([self_query, self_key, self_value, cross_query], axis=1)
    )
    w_outs = ring_gather(jnp.concatenate([self_out.T, cross_out.T], axis=1))
    w_text = ring_gather(jnp.concatenate([cross_key, cross_value], axis=1))
    w_feed = ring_gather(jnp.concatenate([ff_value, ff_gate], axis=1))
    w_down = ring_gather(ff_down.T)
    qkv_full, cq_full = w_self[:, : 3 * own_channels], w_self[:, 3 * own_channels :]
    so_full, co_full = w_outs[:, :own_channels], w_outs[:, own_channels:]
    hidden_own = ff_down.shape[0]

    half_width = C // 2
    wave = dp_index * share + jnp.arange(share, dtype=jnp.int32)
    frequency = jnp.exp(-math.log(10000.0) * (wave % half_width).astype(f32) / half_width)
    angles = steps_all[:, None] * frequency[None, :]
    time_act = jax.nn.silu(
        jnp.where(wave[None, :] < half_width, jnp.cos(angles), jnp.sin(angles))
    ).astype(bf16)
    time_part = jnp.dot(time_act, time_weight, preferred_element_type=f32)
    time_added = lax.all_to_all(
        time_part.reshape(dp_size, slot_count, own_channels), "dp", 0, 0, tiled=True
    ).sum(0)

    masked = latent.astype(f32) * keep
    all_positions = jnp.arange(item_rows, dtype=jnp.int32).reshape(mp_size, 1, local_rows)
    held = (all_positions < filled[None, :, None]).astype(f32).sum(-1) * is_live * per_group
    held_here = jnp.sum(row_mask, axis=1) * per_group
    local_sum = group_sum(masked, per_group)
    local_mean = local_sum / jnp.maximum(held_here, 1.0)[:, None]
    local_center = (masked - spread(local_mean, per_group)) * keep
    local_spread = group_sum(local_center * local_center, per_group)
    stats = share_small(jnp.stack([local_sum, local_spread]), "mp").reshape(
        mp_size, 2, slot_count, GN_GROUPS
    )
    average = jnp.sum(stats[:, 0], axis=0) / counts[:, None]
    means = stats[:, 0] / jnp.maximum(held, 1.0)[:, :, None]
    variance = (
        jnp.sum(stats[:, 1] + held[:, :, None] * (means - average) ** 2, axis=0) / counts[:, None]
    )
    scaling_in = spread(lax.rsqrt(variance + 1e-06), per_group)
    standard_in = (masked - spread(average, per_group)) * scaling_in
    first_act = (jax.nn.silu(standard_in * gain_in_f) * keep).astype(bf16)
    first_all = gather_rows(first_act)

    middle = (
        shift_sum(taps, product(first_all, w_in)) + time_added[:, None, :]
    ) * keep_all
    average_mid = group_sum(middle, per_group) / counts[:, None]
    apart_mid = middle - spread(average_mid, per_group)
    center_mid = apart_mid * keep_all
    scaling_mid = spread(
        lax.rsqrt(group_sum(center_mid * center_mid, per_group) / counts[:, None] + 1e-06),
        per_group,
    )
    standard_mid = apart_mid * scaling_mid
    second_act = (jax.nn.silu(standard_mid * gain_mid_own) * keep_all).astype(bf16)
    second_taps = shift_stack(taps, second_act)
    resnet = (masked + sum_rows(product_back(second_taps, w_out))) * keep

    attend_in, normal_self, scaling_self = norm_rows(resnet, gain_self_f)
    attend_all = gather_rows(attend_in)
    qkv = product(attend_all, qkv_full).astype(bf16)
    query_rows, key_rows, value_rows = jnp.split(qkv, 3, axis=2)
    mixture, self_chances = attend(query_rows, key_rows, value_rows, key_valid)
    after_self = resnet + sum_rows(product_back(mixture, so_full))

    text_pair = product(text_embeds, w_text).astype(bf16)
    text_keys, text_values = jnp.split(text_pair, 2, axis=2)
    cross_in, normal_cross, scaling_cross = norm_rows(after_self, gain_cross_f)
    cross_all = gather_rows(cross_in)
    cross_rows = product(cross_all, cq_full).astype(bf16)
    cross_mix, cross_chances = attend(cross_rows, text_keys, text_values, None)
    after_cross = after_self + sum_rows(product_back(cross_mix, co_full))

    feed_in, normal_feed, scaling_feed = norm_rows(after_cross, gain_feed_f)
    feed_all = gather_rows(feed_in)
    pair_part = product(feed_all, w_feed)
    value_part, gate_part = pair_part[:, :, :hidden_own], pair_part[:, :, hidden_own:]
    below = 0.5 * lax.erfc(-gate_part * math.sqrt(0.5))
    gelu_gate = gate_part * below
    gelu_slope = below + gate_part * jnp.exp(-0.5 * gate_part * gate_part) / math.sqrt(2 * math.pi)
    hidden = (value_part * gelu_gate).astype(bf16)
    output = ((after_cross + sum_rows(product_back(hidden, w_down))) * keep).astype(bf16)

    out_grad = cotangent.astype(f32) * keep
    feed_branch = gather_rows(out_grad.astype(bf16))
    sum_down = ring_scatter(weight_grad(feed_branch, hidden))
    hidden_grad = product(feed_branch, w_down)
    pair_grad = jnp.concatenate(
        [
            (hidden_grad * gelu_gate).astype(bf16),
            (hidden_grad * value_part * gelu_slope).astype(bf16),
        ],
        axis=2,
    )
    sum_feed = ring_scatter(weight_grad(feed_all, pair_grad))
    feed_back = sum_rows(product_back(pair_grad, w_feed))
    feed_dv, grad_gain_feed = norm_rows_back(feed_back, normal_feed, scaling_feed, gain_feed_f)
    cross_grad = out_grad + feed_dv

    cross_branch = gather_rows(cross_grad.astype(bf16))
    grad_cross_out = weight_grad(cross_branch, cross_mix)
    cross_mix_grad = product(cross_branch, co_full).astype(bf16)
    cross_dq, cross_dk, cross_dv = attend_back(
        cross_rows, text_keys, text_values, cross_mix_grad, cross_chances
    )
    grad_cross_query = weight_grad(cross_all, cross_dq)
    sum_text = ring_scatter(weight_grad(text_embeds, jnp.concatenate([cross_dk, cross_dv], axis=2)))
    cross_back = sum_rows(product_back(cross_dq, cq_full))
    cross_dv_rows, grad_gain_cross = norm_rows_back(
        cross_back, normal_cross, scaling_cross, gain_cross_f
    )
    self_grad = cross_grad + cross_dv_rows

    self_branch = gather_rows(self_grad.astype(bf16))
    grad_self_out = weight_grad(self_branch, mixture)
    mixture_grad = product(self_branch, so_full).astype(bf16)
    qkv_grad = jnp.concatenate(
        attend_back(query_rows, key_rows, value_rows, mixture_grad, self_chances), axis=2
    )
    sum_self = ring_scatter(
        jnp.concatenate([weight_grad(attend_all, qkv_grad), grad_cross_query], axis=1)
    )
    sum_outs = ring_scatter(jnp.concatenate([grad_self_out, grad_cross_out], axis=1))
    self_back = sum_rows(product_back(qkv_grad, qkv_full))
    self_dv_rows, grad_gain_self = norm_rows_back(self_back, normal_self, scaling_self, gain_self_f)
    resnet_grad = (self_grad + self_dv_rows) * keep

    resnet_branch = gather_rows(resnet_grad.astype(bf16))
    sum_out = ring_scatter(weight_grad(resnet_branch, second_taps))
    second_grad = shift_sum_back(taps, product(resnet_branch, w_out))
    mid_slope = silu_back(standard_mid * gain_mid_own, second_grad * keep_all)
    mid_gain_part = jnp.sum(mid_slope * standard_mid, axis=(0, 1))
    hat_mid = mid_slope * gain_mid_own
    mid_a = spread(group_sum(hat_mid, per_group) / counts[:, None], per_group)
    mid_b = spread(group_sum(hat_mid * standard_mid, per_group) / counts[:, None], per_group)
    middle_grad = (
        scaling_mid * (hat_mid - (mid_a + standard_mid * mid_b)) * keep_all
    ).astype(bf16)

    time_sum = jnp.sum(middle_grad.astype(f32), axis=1)
    time_sum_all = share_small(time_sum, "dp").reshape(-1, own_channels)
    grad_time = jnp.einsum(
        "sa,sb->ab",
        time_act.astype(f32),
        time_sum_all,
        precision=highest,
        preferred_element_type=f32,
    )

    middle_taps = shift_stack_back(taps, middle_grad)
    sum_in = ring_scatter(weight_grad(first_all, middle_taps))
    first_grad = sum_rows(product_back(middle_taps, w_in))
    in_slope = silu_back(standard_in * gain_in_f, first_grad * keep)
    in_gain_part = jnp.sum(in_slope * standard_in, axis=(0, 1))
    hat_in = in_slope * gain_in_f
    in_a, in_b = lax.psum(
        (group_sum(hat_in, per_group), group_sum(hat_in * standard_in, per_group)), "mp"
    )
    in_a = spread(in_a / counts[:, None], per_group)
    in_b = spread(in_b / counts[:, None], per_group)
    grouped_grad = scaling_in * (hat_in - (in_a + standard_in * in_b))
    latent_grad = ((resnet_grad + grouped_grad) * keep).astype(bf16)

    mid_gain_whole = lax.dynamic_update_slice_in_dim(
        jnp.zeros((channels,), f32), mid_gain_part, channel_start, 0
    )
    gain_parts = jnp.stack(
        [in_gain_part, mid_gain_whole, grad_gain_self, grad_gain_cross, grad_gain_feed]
    )
    gain_parts = jnp.swapaxes(gain_parts.reshape(5, dp_size, share), 0, 1)
    gain_parts = jnp.broadcast_to(gain_parts[:, None], (dp_size, mp_size, 5, share))
    gain_sums = lax.all_to_all(
        gain_parts.reshape(dp_size * mp_size, 5, share), ("dp", "mp"), 0, 0, tiled=True
    ).sum(0)

    return (
        output,
        latent_grad,
        jnp.swapaxes(sum_in.reshape(share, TAPS, own_channels), 0, 1).reshape(conv_in.shape),
        jnp.transpose(sum_out.reshape(share, TAPS, own_channels), (1, 2, 0)).reshape(
            conv_out.shape
        ),
        grad_time,
        sum_self[:, :own_channels],
        sum_self[:, own_channels : 2 * own_channels],
        sum_self[:, 2 * own_channels : 3 * own_channels],
        sum_outs[:, :own_channels].T,
        sum_self[:, 3 * own_channels :],
        sum_text[:, :own_channels],
        sum_text[:, own_channels:],
        sum_outs[:, own_channels:].T,
        sum_feed[:, :hidden_own],
        sum_feed[:, hidden_own:],
        sum_down.T,
        gain_sums[0],
        gain_sums[1],
        gain_sums[2],
        gain_sums[3],
        gain_sums[4],
    )


def solution(mesh):
    in_specs = (
        P("dp", "mp", None),
        P("dp", None, None),
        P("dp", "mp", None),
        P("dp"),
        P("dp"),
        P("dp"),
        P(None, None, "dp", "mp"),
        P(None, None, "mp", "dp"),
        P("dp", "mp"),
        P("dp", "mp"),
        P("dp", "mp"),
        P("dp", "mp"),
        P("mp", "dp"),
        P("dp", "mp"),
        P("dp", "mp"),
        P("dp", "mp"),
        P("mp", "dp"),
        P("dp", "mp"),
        P("dp", "mp"),
        P("mp", "dp"),
        P("dp"),
        P("dp"),
        P("dp"),
        P("dp"),
        P("dp"),
    )
    out_specs = (
        P("dp", "mp", None),
        P("dp", "mp", None),
        P(None, None, "dp", "mp"),
        P(None, None, "mp", "dp"),
        P("dp", "mp"),
        P("dp", "mp"),
        P("dp", "mp"),
        P("dp", "mp"),
        P("mp", "dp"),
        P("dp", "mp"),
        P("dp", "mp"),
        P("dp", "mp"),
        P("mp", "dp"),
        P("dp", "mp"),
        P("dp", "mp"),
        P("mp", "dp"),
        P("dp"),
        P("dp"),
        P("dp"),
        P("dp"),
        P("dp"),
    )
    return jax.shard_map(body, mesh=mesh, in_specs=in_specs, out_specs=out_specs, check_vma=False)
```

```python
import math

import jax
import jax.numpy as jnp
from jax import lax
from jax.experimental.layout import Layout, with_layout_constraint
from jax.sharding import PartitionSpec as P

C = 1280
HEAD_DIM = 64
GN_GROUPS = 32
SIDE = 16
TAPS = 9

highest = lax.Precision.HIGHEST
f32 = jnp.float32
bf16 = jnp.bfloat16


def ring_order(size):
    return list(range(0, size, 2)) + list(range(size - 1, 0, -2))


def ring_pairs(size):
    order = ring_order(size)
    right = [(order[i], order[(i + 1) % size]) for i in range(size)]
    return right, [(b, a) for a, b in right]


def ring_place(size):
    order = ring_order(size)
    place = jnp.array([order.index(i) for i in range(size)], jnp.int32)
    return jnp.array(order, jnp.int32), place[lax.axis_index("dp")]


class Gathered:
    def __init__(self, ring, pack, *parts):
        self.ring, self.pack, self.parts, self.taken = ring, pack, parts, 0

    def put(self, part, away, start):
        place = (self.ring.owner(away), jnp.int32(start), jnp.int32(0))
        self.whole = lax.dynamic_update_slice(self.whole, part[None], place)

    def begin(self):
        ring = self.ring
        if not ring.whole:
            self.whole = lax.all_gather(self.pack(*self.parts), "dp", axis=0, tiled=True)
            return
        zero = jnp.zeros((), self.parts[0].dtype)
        parts = self.parts
        if ring.last:
            zero, *parts = ring.hold(zero, *parts)
        self.block = self.pack(*parts)
        self.whole = jnp.broadcast_to(zero, (ring.size,) + self.block.shape)
        self.put(self.block, 0, 0)
        self.from_left = self.from_right = self.block

    def step(self):
        ring = self.ring
        if not ring.whole:
            return
        self.taken += 1
        size = ring.size
        rows, columns = self.block.shape
        if self.taken < size // 2:
            self.from_left, self.from_right = ring.step(self.from_left, self.from_right)
            self.put(self.from_left, size - self.taken, 0)
            self.put(self.from_right, self.taken, 0)
        else:
            half = rows // 2
            first, second = ring.step(self.from_left[:half], self.from_right[half:])
            self.put(first, size // 2, 0)
            self.put(second, size // 2, half)
            self.whole = self.whole.reshape(size * rows, columns)


class Scattered:
    def __init__(self, ring, *grads):
        self.ring, self.taken = ring, 0
        if not ring.whole:
            parts = [lax.psum_scatter(g, "dp", scatter_dimension=0, tiled=True) for g in grads]
            self.part = jnp.concatenate(parts).astype(f32)
            return
        self.blocks = [g.reshape(ring.size, -1, g.shape[1]) for g in grads]

    def own(self, away):
        place = self.ring.owner(away)
        return jnp.concatenate(
            [lax.dynamic_index_in_dim(b, place, 0, keepdims=False) for b in self.blocks]
        )

    def step(self):
        ring = self.ring
        if not ring.whole:
            return
        size = ring.size
        half = sum(b.shape[1] for b in self.blocks) // 2
        away = size // 2 - self.taken
        self.taken += 1
        ahead, behind = self.own(away), self.own(size - away)
        if self.taken == 1:
            ahead, behind = ahead[:half], behind[half:]
        elif self.taken == 2:
            ahead = jnp.concatenate(
                [(ahead[:half].astype(f32) + self.from_left).astype(bf16), ahead[half:]]
            )
            behind = jnp.concatenate(
                [behind[:half], (behind[half:].astype(f32) + self.from_right).astype(bf16)]
            )
        else:
            ahead = (ahead.astype(f32) + self.from_left).astype(bf16)
            behind = (behind.astype(f32) + self.from_right).astype(bf16)
        self.from_left, self.from_right = ring.step(by_rows(ahead), by_rows(behind))
        if away == 1:
            self.part = (
                self.own(0).astype(f32)
                + self.from_left.astype(f32)
                + self.from_right.astype(f32)
            )


class Ring:
    def __init__(self):
        self.size = lax.axis_size("dp")
        self.whole = self.size == 8
        self.last = ()
        if self.whole:
            self.right, self.left = ring_pairs(self.size)
            self.order, self.place = ring_place(self.size)

    def step(self, to_right, to_left):
        if self.last:
            to_right = lax.optimization_barrier((to_right, self.last[0]))[0]
            to_left = lax.optimization_barrier((to_left, self.last[1]))[0]
        self.last = (
            lax.ppermute(to_right, "dp", self.right),
            lax.ppermute(to_left, "dp", self.left),
        )
        return self.last

    def hold(self, *values):
        held = lax.optimization_barrier(tuple(values) + self.last)[: len(values)]
        return held[0] if len(values) == 1 else held

    def owner(self, away):
        return self.order[(self.place + away) % self.size]


def share_small(values, axis):
    size = lax.axis_size(axis)
    return lax.all_to_all(
        jnp.broadcast_to(values[None], (size,) + values.shape), axis, 0, 0, tiled=True
    )


def mp_bits():
    me = lax.axis_index("mp")
    return me % 2, me // 2


NEAR = [(0, 1), (1, 0), (2, 3), (3, 2)]
FAR = [(0, 2), (2, 0), (1, 3), (3, 1)]


def gather_rows(values):
    near_bit, far_bit = mp_bits()
    far = lax.ppermute(values, "mp", FAR)
    near = lax.ppermute(values, "mp", NEAR)
    both = lax.ppermute(far, "mp", NEAR)

    def pair(mine, other, bit):
        return jnp.concatenate(
            [jnp.where(bit == 0, mine, other), jnp.where(bit == 0, other, mine)], axis=1
        )

    return pair(pair(values, near, near_bit), pair(far, both, near_bit), far_bit)


def sum_rows(values, items):
    near_bit, far_bit = mp_bits()
    columns = values.shape[-1]
    parts = values.reshape(items, 2, 2, -1, columns)

    def near_part(bit):
        return lax.dynamic_index_in_dim(parts, bit, 2, keepdims=False)

    got = lax.ppermute(near_part(1 - near_bit).astype(bf16), "mp", NEAR)
    held = near_part(near_bit).astype(f32) + got.astype(f32)

    def far_part(bit):
        return lax.dynamic_index_in_dim(held, bit, 1, keepdims=False)

    got = lax.ppermute(far_part(1 - far_bit).astype(bf16), "mp", FAR)
    return far_part(far_bit) + got.astype(f32)


def by_rows(values):
    return with_layout_constraint(values, Layout(major_to_minor=tuple(range(values.ndim))))


def flat(values):
    return values.reshape(-1, values.shape[-1])


def product(former, latter):
    return jnp.dot(former, latter, preferred_element_type=f32)


def product_back(former, latter):
    return lax.dot_general(former, latter, (((1,), (1,)), ((), ())), preferred_element_type=f32)


def product_down(former, latter):
    return lax.dot_general(former, latter, (((0,), (0,)), ((), ())), preferred_element_type=f32)


def weight_grad(former, latter):
    return by_rows(product_down(former, latter).astype(bf16))


def tap_sources(widths, item_rows):
    row = jnp.arange(item_rows, dtype=jnp.int32)
    step = jnp.arange(TAPS, dtype=jnp.int32)
    row_step, column_step = step // 3 - 1, step % 3 - 1
    column = row[None, :] % widths[:, None]
    beside = column[:, None, :] + column_step[None, :, None]
    usable = (beside >= 0) & (beside < widths[:, None, None])
    source = (
        row[None, None, :]
        + row_step[None, :, None] * widths[:, None, None]
        + column_step[None, :, None]
    )
    return jnp.where(usable, source, -1)


def tap_matrices(widths, item_rows):
    source = tap_sources(widths, item_rows)
    row = jnp.arange(item_rows, dtype=jnp.int32)
    tall = (source[:, :, :, None] == row).astype(bf16)
    tall = [by_rows(one.reshape(TAPS * item_rows, item_rows)) for one in tall]
    by_row = jnp.swapaxes(source, 1, 2)
    wide = (by_row[:, :, :, None] == row).astype(bf16)
    wide = [by_rows(one.reshape(item_rows, TAPS * item_rows)) for one in wide]
    return tall, wide


def items_of(values, count):
    rows = values.shape[0] // count
    return [values[i * rows : (i + 1) * rows] for i in range(count)]


def beside(stacked):
    rows = stacked.shape[0] // TAPS
    return jnp.concatenate([stacked[t * rows : (t + 1) * rows] for t in range(TAPS)], axis=1)


def below(values):
    columns = values.shape[1] // TAPS
    return jnp.concatenate(
        [values[:, t * columns : (t + 1) * columns] for t in range(TAPS)], axis=0
    )


def shift_stack(tall, values):
    return by_rows(
        jnp.concatenate(
            [
                beside(product(tap, item).astype(bf16))
                for tap, item in zip(tall, items_of(values, len(tall)))
            ]
        )
    )


def shift_stack_back(wide, values):
    return by_rows(
        jnp.concatenate(
            [
                beside(product_down(tap, item).astype(bf16))
                for tap, item in zip(wide, items_of(values, len(wide)))
            ]
        )
    )


def shift_sum(wide, values):
    return jnp.stack(
        [product(tap, below(item)) for tap, item in zip(wide, items_of(values, len(wide)))]
    )


def shift_sum_back(tall, values):
    return jnp.stack(
        [product_down(tap, below(item)) for tap, item in zip(tall, items_of(values, len(tall)))]
    )


def norm_rows(hidden, factor):
    center = hidden - jnp.mean(hidden, axis=-1, keepdims=True)
    scaling = lax.rsqrt(jnp.mean(center * center, axis=-1, keepdims=True) + 1e-05)
    normal = center * scaling
    return ((normal * factor).astype(bf16), normal, scaling)


def norm_rows_back(gradient, normal, scaling, factor):
    scaled = gradient * factor
    offset = jnp.mean(scaled, axis=-1, keepdims=True)
    slopes = jnp.mean(scaled * normal, axis=-1, keepdims=True)
    return (scaling * (scaled - offset - normal * slopes), jnp.sum(gradient * normal, axis=(0, 1)))


def group_sum(values, per_group):
    rows_summed = jnp.sum(values, axis=1)
    return rows_summed.reshape(values.shape[0], values.shape[2] // per_group, per_group).sum(-1)


def spread(values, per_group):
    return jnp.repeat(values, per_group, axis=-1)[:, None, :]


def silu_back(scaled, gradient):
    share = jax.nn.sigmoid(scaled)
    return gradient * share * (1.0 + scaled * (1.0 - share))


def split_heads(values):
    return values.reshape(values.shape[0], values.shape[1], values.shape[2] // HEAD_DIM, HEAD_DIM)


def attend(query_rows, key_rows, value_rows, key_valid):
    scores = jnp.einsum(
        "sqhd,skhd->shqk",
        split_heads(query_rows),
        split_heads(key_rows),
        preferred_element_type=f32,
    ) * HEAD_DIM ** (-0.5)
    if key_valid is not None:
        scores = jnp.where(key_valid[:, None, None, :], scores, -1e30)
    exponent = jnp.exp(scores - jnp.max(scores, axis=-1, keepdims=True))
    chances = exponent / jnp.sum(exponent, axis=-1, keepdims=True)
    mixture = jnp.einsum(
        "shqk,skhd->sqhd",
        chances.astype(bf16),
        split_heads(value_rows),
        preferred_element_type=f32,
    )
    return mixture.reshape(query_rows.shape).astype(bf16), chances


def attend_back(query_rows, key_rows, value_rows, mixture_grad, chances):
    query_heads = split_heads(query_rows)
    key_heads = split_heads(key_rows)
    value_heads = split_heads(value_rows)
    grad_heads = split_heads(mixture_grad)
    value_grad = jnp.einsum(
        "shqk,sqhd->skhd", chances.astype(bf16), grad_heads, preferred_element_type=f32
    )
    share_grad = jnp.einsum(
        "sqhd,skhd->shqk", grad_heads, value_heads, preferred_element_type=f32
    )
    inner_sum = jnp.sum(chances * share_grad, axis=-1, keepdims=True)
    score_grad = (chances * (share_grad - inner_sum)).astype(bf16)
    query_grad = jnp.einsum(
        "shqk,skhd->sqhd", score_grad, key_heads, preferred_element_type=f32
    ) * HEAD_DIM ** (-0.5)
    key_grad = jnp.einsum(
        "shqk,sqhd->skhd", score_grad, query_heads, preferred_element_type=f32
    ) * HEAD_DIM ** (-0.5)
    return (
        query_grad.reshape(query_rows.shape).astype(bf16),
        key_grad.reshape(key_rows.shape).astype(bf16),
        value_grad.reshape(value_rows.shape).astype(bf16),
    )


def body(
    latent,
    text_embeds,
    cotangent,
    item_count,
    bucket,
    timestep,
    conv_in,
    conv_out,
    time_weight,
    self_query,
    self_key,
    self_value,
    self_out,
    cross_query,
    cross_key,
    cross_value,
    cross_out,
    ff_value,
    ff_gate,
    ff_down,
    gn_in_gain,
    gn_mid_gain,
    self_gain,
    cross_gain,
    ff_gain,
):
    slot_count, local_rows, channels = latent.shape
    dp_size, mp_size = lax.axis_size("dp"), lax.axis_size("mp")
    item_rows = local_rows * mp_size
    per_group = channels // GN_GROUPS
    own_channels = conv_in.shape[3]
    share = conv_in.shape[2]
    dp_index, mp_index = lax.axis_index("dp"), lax.axis_index("mp")
    is_live = (jnp.arange(slot_count, dtype=jnp.int32) < item_count[0]).astype(f32)
    widths = jnp.where(
        bucket == 0, SIDE, jnp.where(bucket == 1, 5 * SIDE // 4, 3 * SIDE // 2)
    ).astype(jnp.int32)
    heights = jnp.where(
        bucket == 0, SIDE, jnp.where(bucket == 1, 3 * SIDE // 4, 5 * SIDE // 8)
    ).astype(jnp.int32)
    filled = widths * heights
    position = mp_index * local_rows + jnp.arange(local_rows, dtype=jnp.int32)
    row_mask = (position[None, :] < filled[:, None]).astype(f32) * is_live[:, None]
    key_valid = jnp.arange(item_rows, dtype=jnp.int32)[None, :] < filled[:, None]
    full_mask = key_valid.astype(f32) * is_live[:, None]
    keep = row_mask[:, :, None]
    keep_all = full_mask[:, :, None]
    counts = filled.astype(f32) * per_group
    channel_start = mp_index * own_channels
    ring = Ring()

    def rows3(values):
        return values.reshape(slot_count, item_rows, values.shape[-1])

    def own_sum(values):
        return sum_rows(values, slot_count)

    def across(*parts):
        return jnp.concatenate(parts, axis=1)

    g_in = Gathered(ring, lambda k: across(*[k[t // 3, t % 3] for t in range(TAPS)]), conv_in)
    g_out = Gathered(ring, lambda k: across(*[k[t // 3, t % 3].T for t in range(TAPS)]), conv_out)
    g_self = Gathered(
        ring,
        lambda q, k, v, c, s, o: across(q, k, v, c, s.T, o.T),
        self_query,
        self_key,
        self_value,
        cross_query,
        self_out,
        cross_out,
    )
    g_text = Gathered(ring, across, cross_key, cross_value)
    g_feed = Gathered(ring, across, ff_value, ff_gate)
    g_down = Gathered(ring, lambda down: down.T, ff_down)
    hidden_own = ff_down.shape[0]

    g_in.begin()
    g_in.step()
    gain_parts = jnp.stack([gn_in_gain, gn_mid_gain, self_gain, cross_gain, ff_gain]).astype(f32)
    small = jnp.concatenate([gain_parts.reshape(-1), timestep.astype(f32)])
    small_all = share_small(small, "dp")
    gains = small_all[:, : 5 * share].reshape(dp_size, 5, share)
    gains = jnp.swapaxes(gains, 0, 1).reshape(5, channels)
    gain_in_f, gain_self_f, gain_cross_f, gain_feed_f = gains[0], gains[2], gains[3], gains[4]
    gain_mid_own = lax.dynamic_slice_in_dim(gains[1], channel_start, own_channels)
    steps_all = small_all[:, 5 * share :].reshape(-1)
    latent, gain_in_f, shift_widths = ring.hold(latent, gain_in_f, widths)
    g_in.step()

    masked = latent.astype(f32) * keep
    all_positions = jnp.arange(item_rows, dtype=jnp.int32).reshape(mp_size, 1, local_rows)
    held = (all_positions < filled[None, :, None]).astype(f32).sum(-1) * is_live * per_group
    held_here = jnp.sum(row_mask, axis=1) * per_group
    local_sum = group_sum(masked, per_group)
    local_mean = local_sum / jnp.maximum(held_here, 1.0)[:, None]
    local_center = (masked - spread(local_mean, per_group)) * keep
    local_spread = group_sum(local_center * local_center, per_group)
    stats = share_small(jnp.stack([local_sum, local_spread]), "mp").reshape(
        mp_size, 2, slot_count, GN_GROUPS
    )
    stats, steps_all, cotangent, shift_widths = ring.hold(
        stats, steps_all, cotangent, shift_widths
    )
    g_in.step()
    average = jnp.sum(stats[:, 0], axis=0) / counts[:, None]
    means = stats[:, 0] / jnp.maximum(held, 1.0)[:, :, None]
    variance = (
        jnp.sum(stats[:, 1] + held[:, :, None] * (means - average) ** 2, axis=0) / counts[:, None]
    )
    scaling_in = spread(lax.rsqrt(variance + 1e-06), per_group)
    standard_in = (masked - spread(average, per_group)) * scaling_in
    first_act = (jax.nn.silu(standard_in * gain_in_f) * keep).astype(bf16)
    first_all = flat(gather_rows(first_act))
    first_all, steps_all, cotangent, shift_widths = ring.hold(
        first_all, steps_all, cotangent, shift_widths
    )
    tall, wide = tap_matrices(shift_widths, item_rows)
    g_out.begin()
    g_in.step()

    half_width = C // 2
    wave = dp_index * share + jnp.arange(share, dtype=jnp.int32)
    frequency = jnp.exp(-math.log(10000.0) * (wave % half_width).astype(f32) / half_width)
    angles = steps_all[:, None] * frequency[None, :]
    time_act = jax.nn.silu(
        jnp.where(wave[None, :] < half_width, jnp.cos(angles), jnp.sin(angles))
    ).astype(bf16)
    time_part = jnp.dot(time_act, time_weight, preferred_element_type=f32)
    time_added = lax.all_to_all(
        time_part.reshape(dp_size, slot_count, own_channels), "dp", 0, 0, tiled=True
    ).sum(0)
    w_in = g_in.whole

    g_out.step()
    first_taps = product(first_all, w_in).astype(bf16)
    first_taps, time_added, cotangent, text_embeds = ring.hold(
        first_taps, time_added, cotangent, text_embeds
    )
    g_out.step()
    middle = (shift_sum(wide, first_taps) + time_added[:, None, :]) * keep_all
    average_mid = group_sum(middle, per_group) / counts[:, None]
    apart_mid = middle - spread(average_mid, per_group)
    center_mid = apart_mid * keep_all
    scaling_mid = spread(
        lax.rsqrt(group_sum(center_mid * center_mid, per_group) / counts[:, None] + 1e-06),
        per_group,
    )
    standard_mid = apart_mid * scaling_mid
    standard_mid, cotangent, text_embeds = ring.hold(standard_mid, cotangent, text_embeds)
    g_out.step()
    second_act = (jax.nn.silu(standard_mid * gain_mid_own) * keep_all).astype(bf16)
    second_taps = shift_stack(tall, flat(second_act))
    second_taps, cotangent, text_embeds = ring.hold(second_taps, cotangent, text_embeds)
    g_self.begin()
    g_out.step()
    out_grad = cotangent.astype(f32) * keep
    feed_branch = flat(gather_rows(out_grad.astype(bf16)))
    w_out = g_out.whole
    g_self.step()
    second_out = product_back(second_taps, w_out)
    second_out, text_embeds = ring.hold(second_out, text_embeds)
    g_self.step()
    resnet = (masked + own_sum(second_out)) * keep

    attend_in, normal_self, scaling_self = norm_rows(resnet, gain_self_f)
    attend_in = ring.hold(attend_in)
    g_self.step()
    attend_all = flat(gather_rows(attend_in))
    attend_all = ring.hold(attend_all)
    g_text.begin()
    g_self.step()
    w_self = g_self.whole
    qkv_full = w_self[:, : 3 * own_channels]
    cq_full = w_self[:, 3 * own_channels : 4 * own_channels]
    so_full = w_self[:, 4 * own_channels : 5 * own_channels]
    co_full = w_self[:, 5 * own_channels :]
    g_text.step()
    qkv = product(attend_all, qkv_full).astype(bf16)
    qkv = rows3(ring.hold(qkv))
    g_text.step()
    query_rows, key_rows, value_rows = jnp.split(qkv, 3, axis=2)
    mixture, self_chances = attend(query_rows, key_rows, value_rows, key_valid)
    self_part = product_back(flat(mixture), so_full)
    self_part = ring.hold(self_part)
    g_text.step()
    g_feed.begin()
    g_text.step()
    w_text = g_text.whole
    after_self = resnet + own_sum(self_part)
    g_feed.step()

    text_rows = flat(text_embeds)
    text_pair = product(text_rows, w_text).astype(bf16).reshape(slot_count, -1, 2 * own_channels)
    text_keys, text_values = jnp.split(text_pair, 2, axis=2)
    cross_in, normal_cross, scaling_cross = norm_rows(after_self, gain_cross_f)
    cross_all = flat(gather_rows(cross_in))
    cross_all = ring.hold(cross_all)
    g_feed.step()
    cross_rows = rows3(product(cross_all, cq_full).astype(bf16))
    cross_mix, cross_chances = attend(cross_rows, text_keys, text_values, None)
    cross_part = product_back(flat(cross_mix), co_full)
    cross_part = ring.hold(cross_part)
    g_feed.step()
    after_cross = after_self + own_sum(cross_part)

    feed_in, normal_feed, scaling_feed = norm_rows(after_cross, gain_feed_f)
    feed_in = ring.hold(feed_in)
    g_down.begin()
    g_feed.step()
    feed_all = flat(gather_rows(feed_in))
    w_feed = g_feed.whole
    g_down.step()
    pair_part = product(feed_all, w_feed)
    pair_part = ring.hold(pair_part)
    g_down.step()
    value_part, gate_part = pair_part[:, :hidden_own], pair_part[:, hidden_own:]
    lower = 0.5 * lax.erfc(-gate_part * math.sqrt(0.5))
    gelu_gate = gate_part * lower
    gelu_slope = lower + gate_part * jnp.exp(-0.5 * gate_part * gate_part) / math.sqrt(2 * math.pi)
    hidden = (value_part * gelu_gate).astype(bf16)
    hidden = ring.hold(hidden)
    g_down.step()
    s_down = Scattered(ring, weight_grad(feed_branch, hidden))
    g_down.step()
    w_down = g_down.whole

    s_down.step()
    hidden_grad = product(feed_branch, w_down)
    pair_grad = jnp.concatenate(
        [
            (hidden_grad * gelu_gate).astype(bf16),
            (hidden_grad * value_part * gelu_slope).astype(bf16),
        ],
        axis=1,
    )
    pair_grad = ring.hold(pair_grad)
    s_down.step()
    feed_part = product_back(pair_grad, w_feed)
    feed_part = ring.hold(feed_part)
    s_down.step()
    s_feed = Scattered(ring, weight_grad(feed_all, pair_grad))
    feed_back = own_sum(feed_part)
    feed_back = ring.hold(feed_back)
    s_down.step()
    feed_dv, grad_gain_feed = norm_rows_back(feed_back, normal_feed, scaling_feed, gain_feed_f)
    cross_grad = out_grad + feed_dv
    cross_branch = flat(gather_rows(cross_grad.astype(bf16)))
    cross_branch = ring.hold(cross_branch)
    s_feed.step()

    cross_mix_grad = rows3(product(cross_branch, co_full).astype(bf16))
    cross_dq, cross_dk, cross_dv = attend_back(
        cross_rows, text_keys, text_values, cross_mix_grad, cross_chances
    )
    cross_dq = flat(cross_dq)
    cross_dq, cross_dk, cross_dv = ring.hold(cross_dq, cross_dk, cross_dv)
    s_feed.step()
    cross_back = own_sum(product_back(cross_dq, cq_full))
    grad_cross_out = weight_grad(cross_branch, flat(cross_mix))
    grad_cross_query = weight_grad(cross_all, cross_dq)
    s_cross = Scattered(
        ring,
        weight_grad(text_rows, flat(jnp.concatenate([cross_dk, cross_dv], axis=2))),
        jnp.concatenate([grad_cross_query, grad_cross_out], axis=1),
    )
    cross_back = ring.hold(cross_back)
    s_feed.step()
    cross_dv_rows, grad_gain_cross = norm_rows_back(
        cross_back, normal_cross, scaling_cross, gain_cross_f
    )
    self_grad = cross_grad + cross_dv_rows

    self_branch = flat(gather_rows(self_grad.astype(bf16)))
    mixture_grad = product(self_branch, so_full).astype(bf16)
    mixture_grad = rows3(ring.hold(mixture_grad))
    s_feed.step()
    qkv_grad = flat(
        jnp.concatenate(
            attend_back(query_rows, key_rows, value_rows, mixture_grad, self_chances), axis=2
        )
    )
    self_back = own_sum(product_back(qkv_grad, qkv_full))
    self_back = ring.hold(self_back)
    s_cross.step()
    self_dv_rows, grad_gain_self = norm_rows_back(self_back, normal_self, scaling_self, gain_self_f)
    resnet_grad = (self_grad + self_dv_rows) * keep
    resnet_grad = ring.hold(resnet_grad)
    s_cross.step()
    resnet_branch = flat(gather_rows(resnet_grad.astype(bf16)))
    resnet_branch = ring.hold(resnet_branch)
    s_cross.step()

    second_parts = product(resnet_branch, w_out).astype(bf16)
    second_parts = ring.hold(second_parts)
    s_cross.step()
    grad_self_out = weight_grad(self_branch, flat(mixture))
    s_self = Scattered(
        ring, jnp.concatenate([weight_grad(attend_all, qkv_grad), grad_self_out], axis=1)
    )
    second_grad = shift_sum_back(tall, second_parts)
    second_grad = ring.hold(second_grad)
    s_self.step()
    s_out = Scattered(ring, weight_grad(resnet_branch, second_taps))
    mid_slope = silu_back(standard_mid * gain_mid_own, second_grad * keep_all)
    mid_gain_part = jnp.sum(mid_slope * standard_mid, axis=(0, 1))
    hat_mid = mid_slope * gain_mid_own
    mid_a = spread(group_sum(hat_mid, per_group) / counts[:, None], per_group)
    mid_b = spread(group_sum(hat_mid * standard_mid, per_group) / counts[:, None], per_group)
    middle_grad = (
        scaling_mid * (hat_mid - (mid_a + standard_mid * mid_b)) * keep_all
    ).astype(bf16)
    middle_grad = ring.hold(middle_grad)
    s_self.step()
    middle_taps = shift_stack_back(wide, flat(middle_grad))
    middle_taps = ring.hold(middle_taps)
    s_self.step()
    first_part = product_back(middle_taps, w_in)
    first_part = ring.hold(first_part)
    s_self.step()
    s_in = Scattered(ring, weight_grad(first_all, middle_taps))
    first_grad = own_sum(first_part)
    first_grad, hidden = ring.hold(first_grad, hidden)
    s_out.step()

    time_sum = jnp.sum(middle_grad.astype(f32), axis=1)
    time_sum_all = share_small(time_sum, "dp").reshape(-1, own_channels)
    grad_time = jnp.einsum(
        "sa,sb->ab",
        time_act.astype(f32),
        time_sum_all,
        precision=highest,
        preferred_element_type=f32,
    )

    in_slope = silu_back(standard_in * gain_in_f, first_grad * keep)
    in_gain_part = jnp.sum(in_slope * standard_in, axis=(0, 1))
    hat_in = in_slope * gain_in_f
    in_a, in_b = lax.psum(
        (group_sum(hat_in, per_group), group_sum(hat_in * standard_in, per_group)), "mp"
    )
    in_a, in_b, grad_time = ring.hold(in_a, in_b, grad_time)
    s_out.step()
    in_a = spread(in_a / counts[:, None], per_group)
    in_b = spread(in_b / counts[:, None], per_group)
    grouped_grad = scaling_in * (hat_in - (in_a + standard_in * in_b))
    latent_grad = ((resnet_grad + grouped_grad) * keep).astype(bf16)
    latent_grad, hidden = ring.hold(latent_grad, hidden)
    s_out.step()
    output = ((after_cross + own_sum(product_back(hidden, w_down))) * keep).astype(bf16)
    output = ring.hold(output)
    s_out.step()
    s_in.step()

    mid_gain_whole = lax.dynamic_update_slice_in_dim(
        jnp.zeros((channels,), f32), mid_gain_part, channel_start, 0
    )
    gain_parts = jnp.stack(
        [in_gain_part, mid_gain_whole, grad_gain_self, grad_gain_cross, grad_gain_feed]
    )
    gain_parts = jnp.swapaxes(gain_parts.reshape(5, dp_size, share), 0, 1)
    gain_parts = jnp.broadcast_to(gain_parts[:, None], (dp_size, mp_size, 5, share))
    gain_sums = lax.all_to_all(
        gain_parts.reshape(dp_size * mp_size, 5, share), ("dp", "mp"), 0, 0, tiled=True
    ).sum(0)
    gain_sums = ring.hold(gain_sums)
    s_in.step()
    s_in.step()
    s_in.step()
    sum_in, sum_out, sum_self = s_in.part, s_out.part, s_self.part
    sum_feed, sum_down = s_feed.part, s_down.part
    text_share = cross_key.shape[0]
    sum_text, sum_cross = s_cross.part[:text_share], s_cross.part[text_share:]

    def tap_part(values, tap):
        return values[:, tap * own_channels : (tap + 1) * own_channels]

    def column_part(values, part):
        return values[:, part * own_channels : (part + 1) * own_channels]

    return (
        output,
        latent_grad,
        jnp.stack([tap_part(sum_in, t) for t in range(TAPS)]).reshape(conv_in.shape),
        jnp.stack([tap_part(sum_out, t).T for t in range(TAPS)]).reshape(conv_out.shape),
        grad_time,
        column_part(sum_self, 0),
        column_part(sum_self, 1),
        column_part(sum_self, 2),
        column_part(sum_self, 3).T,
        column_part(sum_cross, 0),
        column_part(sum_text, 0),
        column_part(sum_text, 1),
        column_part(sum_cross, 1).T,
        sum_feed[:, :hidden_own],
        sum_feed[:, hidden_own:],
        sum_down.T,
        gain_sums[0],
        gain_sums[1],
        gain_sums[2],
        gain_sums[3],
        gain_sums[4],
    )


def solution(mesh):
    in_specs = (
        P("dp", "mp", None),
        P("dp", None, None),
        P("dp", "mp", None),
        P("dp"),
        P("dp"),
        P("dp"),
        P(None, None, "dp", "mp"),
        P(None, None, "mp", "dp"),
        P("dp", "mp"),
        P("dp", "mp"),
        P("dp", "mp"),
        P("dp", "mp"),
        P("mp", "dp"),
        P("dp", "mp"),
        P("dp", "mp"),
        P("dp", "mp"),
        P("mp", "dp"),
        P("dp", "mp"),
        P("dp", "mp"),
        P("mp", "dp"),
        P("dp"),
        P("dp"),
        P("dp"),
        P("dp"),
        P("dp"),
    )
    out_specs = (
        P("dp", "mp", None),
        P("dp", "mp", None),
        P(None, None, "dp", "mp"),
        P(None, None, "mp", "dp"),
        P("dp", "mp"),
        P("dp", "mp"),
        P("dp", "mp"),
        P("dp", "mp"),
        P("mp", "dp"),
        P("dp", "mp"),
        P("dp", "mp"),
        P("dp", "mp"),
        P("mp", "dp"),
        P("dp", "mp"),
        P("dp", "mp"),
        P("mp", "dp"),
        P("dp"),
        P("dp"),
        P("dp"),
        P("dp"),
        P("dp"),
    )
    return jax.shard_map(body, mesh=mesh, in_specs=in_specs, out_specs=out_specs, check_vma=False)
```

```python
import math

import jax
import jax.numpy as jnp
from jax import lax
from jax.experimental.layout import Layout, with_layout_constraint
from jax.sharding import PartitionSpec as P

C = 1280
HEAD_DIM = 64
GN_GROUPS = 32
SIDE = 16
TAPS = 9

highest = lax.Precision.HIGHEST
f32 = jnp.float32
bf16 = jnp.bfloat16


def ring_order(size):
    return list(range(0, size, 2)) + list(range(size - 1, 0, -2))


def ring_pairs(size):
    order = ring_order(size)
    right = [(order[i], order[(i + 1) % size]) for i in range(size)]
    return right, [(b, a) for a, b in right]


def ring_owners(size):
    order = ring_order(size)
    table = [[order[(order.index(i) + away) % size] for away in range(size)] for i in range(size)]
    row = lax.dynamic_slice(
        jnp.array(table, jnp.uint32),
        (lax.axis_index("dp").astype(jnp.uint32), jnp.uint32(0)),
        (1, size),
    )
    return [jnp.minimum(row[0, away], jnp.uint32(size - 1)) for away in range(size)]


class Gathered:
    def __init__(self, ring, pack, *parts):
        self.ring, self.pack, self.parts, self.taken = ring, pack, parts, 0

    def put(self, part, away, start):
        place = (self.ring.owner(away), jnp.uint32(start), jnp.uint32(0))
        self.whole = lax.dynamic_update_slice(self.whole, part[None], place)

    def begin(self):
        ring = self.ring
        if not ring.whole:
            self.whole = lax.all_gather(self.pack(*self.parts), "dp", axis=0, tiled=True)
            return
        zero = jnp.zeros((), self.parts[0].dtype)
        parts = self.parts
        if ring.last:
            zero, *parts = ring.hold(zero, *parts)
        self.block = self.pack(*parts)
        self.whole = jnp.broadcast_to(zero, (ring.size,) + self.block.shape)
        self.put(self.block, 0, 0)
        self.from_left = self.from_right = self.block

    def step(self):
        ring = self.ring
        if not ring.whole:
            return
        self.taken += 1
        size = ring.size
        rows, columns = self.block.shape
        if self.taken < size // 2:
            self.from_left, self.from_right = ring.step(self.from_left, self.from_right)
            self.put(self.from_left, size - self.taken, 0)
            self.put(self.from_right, self.taken, 0)
        else:
            half = rows // 2
            first, second = ring.step(self.from_left[:half], self.from_right[half:])
            self.put(first, size // 2, 0)
            self.put(second, size // 2, half)
            self.whole = self.whole.reshape(size * rows, columns)


class Scattered:
    def __init__(self, ring, *grads):
        self.ring, self.taken = ring, 0
        if not ring.whole:
            parts = [lax.psum_scatter(g, "dp", scatter_dimension=0, tiled=True) for g in grads]
            self.part = jnp.concatenate(parts).astype(f32)
            return
        self.blocks = [g.reshape(ring.size, -1, g.shape[1]) for g in grads]

    def own(self, away):
        place = self.ring.owner(away)
        zero = jnp.uint32(0)
        return jnp.concatenate(
            [
                lax.dynamic_slice(b, (place, zero, zero), (1,) + b.shape[1:])[0]
                for b in self.blocks
            ]
        )

    def step(self):
        ring = self.ring
        if not ring.whole:
            return
        size = ring.size
        half = sum(b.shape[1] for b in self.blocks) // 2
        away = size // 2 - self.taken
        self.taken += 1
        ahead, behind = self.own(away), self.own(size - away)
        if self.taken == 1:
            ahead, behind = ahead[:half], behind[half:]
        elif self.taken == 2:
            ahead = jnp.concatenate(
                [(ahead[:half].astype(f32) + self.from_left).astype(bf16), ahead[half:]]
            )
            behind = jnp.concatenate(
                [behind[:half], (behind[half:].astype(f32) + self.from_right).astype(bf16)]
            )
        else:
            ahead = (ahead.astype(f32) + self.from_left).astype(bf16)
            behind = (behind.astype(f32) + self.from_right).astype(bf16)
        self.from_left, self.from_right = ring.step(by_rows(ahead), by_rows(behind))
        if away == 1:
            self.part = (
                self.own(0).astype(f32)
                + self.from_left.astype(f32)
                + self.from_right.astype(f32)
            )


class Ring:
    def __init__(self):
        self.size = lax.axis_size("dp")
        self.whole = self.size == 8
        self.last = ()
        if self.whole:
            self.right, self.left = ring_pairs(self.size)
            self.owners = ring_owners(self.size)

    def step(self, to_right, to_left):
        if self.last:
            to_right, to_left = lax.optimization_barrier((to_right, to_left, self.last))[:2]
        self.last = (
            lax.ppermute(to_right, "dp", self.right),
            lax.ppermute(to_left, "dp", self.left),
        )
        return self.last

    def hold(self, *values):
        held = lax.optimization_barrier((values, self.last))[0]
        return held[0] if len(values) == 1 else held

    def owner(self, away):
        return self.owners[away % self.size]


def share_small(values, axis):
    size = lax.axis_size(axis)
    return lax.all_to_all(
        jnp.broadcast_to(values[None], (size,) + values.shape), axis, 0, 0, tiled=True
    )


def mp_bits():
    me = lax.axis_index("mp").astype(jnp.uint32)
    return me & 1, me >> 1


NEAR = [(0, 1), (1, 0), (2, 3), (3, 2)]
FAR = [(0, 2), (2, 0), (1, 3), (3, 1)]


def gather_rows(values):
    near_bit, far_bit = mp_bits()
    far = lax.ppermute(values, "mp", FAR)
    near = lax.ppermute(values, "mp", NEAR)
    both = lax.ppermute(far, "mp", NEAR)

    def pair(mine, other, bit):
        return jnp.concatenate(
            [jnp.where(bit == 0, mine, other), jnp.where(bit == 0, other, mine)], axis=1
        )

    return pair(pair(values, near, near_bit), pair(far, both, near_bit), far_bit)


def sum_near(values, items):
    near_bit, _ = mp_bits()
    parts = values.reshape(items, 2, 2, -1, values.shape[-1])

    def near_part(bit):
        zero = jnp.uint32(0)
        sizes = parts.shape[:2] + (1,) + parts.shape[3:]
        return lax.dynamic_slice(parts, (zero, zero, bit, zero, zero), sizes)[:, :, 0]

    got = lax.ppermute(near_part(1 - near_bit).astype(bf16), "mp", NEAR)
    return near_part(near_bit).astype(f32) + got.astype(f32)


def sum_far(held):
    _, far_bit = mp_bits()

    def far_part(bit):
        zero = jnp.uint32(0)
        sizes = held.shape[:1] + (1,) + held.shape[2:]
        return lax.dynamic_slice(held, (zero, bit, zero, zero), sizes)[:, 0]

    got = lax.ppermute(far_part(1 - far_bit).astype(bf16), "mp", FAR)
    return far_part(far_bit) + got.astype(f32)


def by_rows(values):
    return with_layout_constraint(values, Layout(major_to_minor=tuple(range(values.ndim))))


def flat(values):
    return values.reshape(-1, values.shape[-1])


def product(former, latter):
    return jnp.dot(former, latter, preferred_element_type=f32)


def product_back(former, latter):
    return lax.dot_general(former, latter, (((1,), (1,)), ((), ())), preferred_element_type=f32)


def product_down(former, latter):
    return lax.dot_general(former, latter, (((0,), (0,)), ((), ())), preferred_element_type=f32)


def weight_grad(former, latter):
    return by_rows(product_down(former, latter).astype(bf16))


def tap_sources(widths, item_rows):
    row = jnp.arange(item_rows, dtype=jnp.int32)
    step = jnp.arange(TAPS, dtype=jnp.int32)
    row_step, column_step = step // 3 - 1, step % 3 - 1
    column = row[None, :] % widths[:, None]
    beside = column[:, None, :] + column_step[None, :, None]
    usable = (beside >= 0) & (beside < widths[:, None, None])
    source = (
        row[None, None, :]
        + row_step[None, :, None] * widths[:, None, None]
        + column_step[None, :, None]
    )
    return jnp.where(usable, source, -1)


def tap_matrices(widths, item_rows):
    source = tap_sources(widths, item_rows)
    row = jnp.arange(item_rows, dtype=jnp.int32)
    tall = (source[:, :, :, None] == row).astype(bf16)
    tall = [by_rows(one.reshape(TAPS * item_rows, item_rows)) for one in tall]
    by_row = jnp.swapaxes(source, 1, 2)
    wide = (by_row[:, :, :, None] == row).astype(bf16)
    wide = [by_rows(one.reshape(item_rows, TAPS * item_rows)) for one in wide]
    return tall, wide


def items_of(values, count):
    rows = values.shape[0] // count
    return [values[i * rows : (i + 1) * rows] for i in range(count)]


def beside(stacked):
    rows = stacked.shape[0] // TAPS
    return jnp.concatenate([stacked[t * rows : (t + 1) * rows] for t in range(TAPS)], axis=1)


def below(values):
    columns = values.shape[1] // TAPS
    return jnp.concatenate(
        [values[:, t * columns : (t + 1) * columns] for t in range(TAPS)], axis=0
    )


def shift_stack(tall, values):
    return by_rows(
        jnp.concatenate(
            [
                beside(product(tap, item).astype(bf16))
                for tap, item in zip(tall, items_of(values, len(tall)))
            ]
        )
    )


def shift_stack_back(wide, values):
    return by_rows(
        jnp.concatenate(
            [
                beside(product_down(tap, item).astype(bf16))
                for tap, item in zip(wide, items_of(values, len(wide)))
            ]
        )
    )


def shift_sum(wide, values):
    return jnp.stack(
        [product(tap, below(item)) for tap, item in zip(wide, items_of(values, len(wide)))]
    )


def shift_sum_back(tall, values):
    return jnp.stack(
        [product_down(tap, below(item)) for tap, item in zip(tall, items_of(values, len(tall)))]
    )


def norm_rows(hidden, factor):
    center = hidden - jnp.mean(hidden, axis=-1, keepdims=True)
    scaling = lax.rsqrt(jnp.mean(center * center, axis=-1, keepdims=True) + 1e-05)
    normal = center * scaling
    return ((normal * factor).astype(bf16), normal, scaling)


def norm_rows_back(gradient, normal, scaling, factor):
    scaled = gradient * factor
    offset = jnp.mean(scaled, axis=-1, keepdims=True)
    slopes = jnp.mean(scaled * normal, axis=-1, keepdims=True)
    return (scaling * (scaled - offset - normal * slopes), jnp.sum(gradient * normal, axis=(0, 1)))


def group_sum(values, per_group):
    rows_summed = jnp.sum(values, axis=1)
    return rows_summed.reshape(values.shape[0], values.shape[2] // per_group, per_group).sum(-1)


def spread(values, per_group):
    return jnp.repeat(values, per_group, axis=-1)[:, None, :]


def silu_back(scaled, gradient):
    share = jax.nn.sigmoid(scaled)
    return gradient * share * (1.0 + scaled * (1.0 - share))


def split_heads(values):
    return values.reshape(values.shape[0], values.shape[1], values.shape[2] // HEAD_DIM, HEAD_DIM)


def attend(query_rows, key_rows, value_rows, key_valid):
    scores = jnp.einsum(
        "sqhd,skhd->shqk",
        split_heads(query_rows),
        split_heads(key_rows),
        preferred_element_type=f32,
    ) * HEAD_DIM ** (-0.5)
    if key_valid is not None:
        scores = jnp.where(key_valid[:, None, None, :], scores, -1e30)
    exponent = jnp.exp(scores - jnp.max(scores, axis=-1, keepdims=True))
    chances = exponent / jnp.sum(exponent, axis=-1, keepdims=True)
    mixture = jnp.einsum(
        "shqk,skhd->sqhd",
        chances.astype(bf16),
        split_heads(value_rows),
        preferred_element_type=f32,
    )
    return mixture.reshape(query_rows.shape).astype(bf16), chances


def attend_back(query_rows, key_rows, value_rows, mixture_grad, chances):
    query_heads = split_heads(query_rows)
    key_heads = split_heads(key_rows)
    value_heads = split_heads(value_rows)
    grad_heads = split_heads(mixture_grad)
    value_grad = jnp.einsum(
        "shqk,sqhd->skhd", chances.astype(bf16), grad_heads, preferred_element_type=f32
    )
    share_grad = jnp.einsum(
        "sqhd,skhd->shqk", grad_heads, value_heads, preferred_element_type=f32
    )
    inner_sum = jnp.sum(chances * share_grad, axis=-1, keepdims=True)
    score_grad = (chances * (share_grad - inner_sum)).astype(bf16)
    query_grad = jnp.einsum(
        "shqk,skhd->sqhd", score_grad, key_heads, preferred_element_type=f32
    ) * HEAD_DIM ** (-0.5)
    key_grad = jnp.einsum(
        "shqk,sqhd->skhd", score_grad, query_heads, preferred_element_type=f32
    ) * HEAD_DIM ** (-0.5)
    return (
        query_grad.reshape(query_rows.shape).astype(bf16),
        key_grad.reshape(key_rows.shape).astype(bf16),
        value_grad.reshape(value_rows.shape).astype(bf16),
    )


def body(
    latent,
    text_embeds,
    cotangent,
    item_count,
    bucket,
    timestep,
    conv_in,
    conv_out,
    time_weight,
    self_query,
    self_key,
    self_value,
    self_out,
    cross_query,
    cross_key,
    cross_value,
    cross_out,
    ff_value,
    ff_gate,
    ff_down,
    gn_in_gain,
    gn_mid_gain,
    self_gain,
    cross_gain,
    ff_gain,
):
    slot_count, local_rows, channels = latent.shape
    dp_size, mp_size = lax.axis_size("dp"), lax.axis_size("mp")
    item_rows = local_rows * mp_size
    per_group = channels // GN_GROUPS
    own_channels = conv_in.shape[3]
    share = conv_in.shape[2]
    dp_index, mp_index = lax.axis_index("dp"), lax.axis_index("mp")
    ring = Ring()

    def across(*parts):
        return jnp.concatenate(parts, axis=1)

    g_in = Gathered(ring, lambda k: across(*[k[t // 3, t % 3] for t in range(TAPS)]), conv_in)
    g_out = Gathered(ring, lambda k: across(*[k[t // 3, t % 3].T for t in range(TAPS)]), conv_out)
    g_self = Gathered(
        ring,
        lambda q, k, v, c, s, o: across(q, k, v, c, s.T, o.T),
        self_query,
        self_key,
        self_value,
        cross_query,
        self_out,
        cross_out,
    )
    g_text = Gathered(ring, across, cross_key, cross_value)
    g_feed = Gathered(ring, across, ff_value, ff_gate)
    g_down = Gathered(ring, lambda down: down.T, ff_down)
    hidden_own = ff_down.shape[0]

    g_in.begin()
    g_out.begin()
    g_in.step()
    gain_parts = jnp.stack([gn_in_gain, gn_mid_gain, self_gain, cross_gain, ff_gain]).astype(f32)
    small = jnp.concatenate([gain_parts.reshape(-1), timestep.astype(f32)])
    small_all = share_small(small, "dp")
    latent, item_count, bucket, later = ring.hold(
        latent, item_count, bucket, (cotangent, text_embeds)
    )
    g_in.step()

    is_live = (jnp.arange(slot_count, dtype=jnp.int32) < item_count[0]).astype(f32)
    widths = jnp.where(
        bucket == 0, SIDE, jnp.where(bucket == 1, 5 * SIDE // 4, 3 * SIDE // 2)
    ).astype(jnp.int32)
    heights = jnp.where(
        bucket == 0, SIDE, jnp.where(bucket == 1, 3 * SIDE // 4, 5 * SIDE // 8)
    ).astype(jnp.int32)
    filled = widths * heights
    position = mp_index * local_rows + jnp.arange(local_rows, dtype=jnp.int32)
    row_mask = (position[None, :] < filled[:, None]).astype(f32) * is_live[:, None]
    key_valid = jnp.arange(item_rows, dtype=jnp.int32)[None, :] < filled[:, None]
    full_mask = key_valid.astype(f32) * is_live[:, None]
    keep = row_mask[:, :, None]
    keep_all = full_mask[:, :, None]
    counts = filled.astype(f32) * per_group
    channel_start = mp_index * own_channels

    def rows3(values):
        return values.reshape(slot_count, item_rows, values.shape[-1])

    def own_sum(values):
        return sum_far(sum_near(values, slot_count))

    masked = latent.astype(f32) * keep
    all_positions = jnp.arange(item_rows, dtype=jnp.int32).reshape(mp_size, 1, local_rows)
    held = (all_positions < filled[None, :, None]).astype(f32).sum(-1) * is_live * per_group
    held_here = jnp.sum(row_mask, axis=1) * per_group
    local_sum = group_sum(masked, per_group)
    local_mean = local_sum / jnp.maximum(held_here, 1.0)[:, None]
    local_center = (masked - spread(local_mean, per_group)) * keep
    local_spread = group_sum(local_center * local_center, per_group)
    stats = share_small(jnp.stack([local_sum, local_spread]), "mp").reshape(
        mp_size, 2, slot_count, GN_GROUPS
    )
    stats, small_all, later = ring.hold(stats, small_all, later)
    g_in.step()
    gains = small_all[:, : 5 * share].reshape(dp_size, 5, share)
    gains = jnp.swapaxes(gains, 0, 1).reshape(5, channels)
    gain_in_f, gain_self_f, gain_cross_f, gain_feed_f = gains[0], gains[2], gains[3], gains[4]
    gain_mid_own = lax.dynamic_slice_in_dim(gains[1], channel_start, own_channels)
    steps_all = small_all[:, 5 * share :].reshape(-1)
    average = jnp.sum(stats[:, 0], axis=0) / counts[:, None]
    means = stats[:, 0] / jnp.maximum(held, 1.0)[:, :, None]
    variance = (
        jnp.sum(stats[:, 1] + held[:, :, None] * (means - average) ** 2, axis=0) / counts[:, None]
    )
    scaling_in = spread(lax.rsqrt(variance + 1e-06), per_group)
    standard_in = (masked - spread(average, per_group)) * scaling_in
    first_act = (jax.nn.silu(standard_in * gain_in_f) * keep).astype(bf16)
    first_all = flat(gather_rows(first_act))

    half_width = C // 2
    wave = dp_index * share + jnp.arange(share, dtype=jnp.int32)
    frequency = jnp.exp(-math.log(10000.0) * (wave % half_width).astype(f32) / half_width)
    angles = steps_all[:, None] * frequency[None, :]
    time_act = jax.nn.silu(
        jnp.where(wave[None, :] < half_width, jnp.cos(angles), jnp.sin(angles))
    ).astype(bf16)
    time_part = jnp.dot(time_act, time_weight, preferred_element_type=f32)
    first_all, time_part, later = ring.hold(first_all, time_part, later)
    g_in.step()
    first_all, time_part, shift_widths, later = ring.hold(first_all, time_part, widths, later)
    w_in = g_in.whole

    g_out.step()
    first_taps = product(first_all, w_in).astype(bf16)
    cotangent, text_embeds = later
    tall, wide = tap_matrices(shift_widths, item_rows)

    time_added = lax.all_to_all(
        time_part.reshape(dp_size, slot_count, own_channels), "dp", 0, 0, tiled=True
    ).sum(0)
    first_taps, time_added, cotangent, text_embeds = ring.hold(
        first_taps, time_added, cotangent, text_embeds
    )
    g_out.step()
    middle = (shift_sum(wide, first_taps) + time_added[:, None, :]) * keep_all
    middle, cotangent, text_embeds = ring.hold(middle, cotangent, text_embeds)
    g_out.step()
    average_mid = group_sum(middle, per_group) / counts[:, None]
    apart_mid = middle - spread(average_mid, per_group)
    center_mid = apart_mid * keep_all
    scaling_mid = spread(
        lax.rsqrt(group_sum(center_mid * center_mid, per_group) / counts[:, None] + 1e-06),
        per_group,
    )
    standard_mid = apart_mid * scaling_mid
    second_act = (jax.nn.silu(standard_mid * gain_mid_own) * keep_all).astype(bf16)
    second_act, cotangent, text_embeds = ring.hold(second_act, cotangent, text_embeds)
    g_self.begin()
    g_out.step()
    second_taps = shift_stack(tall, flat(second_act))
    second_taps, cotangent, text_embeds = ring.hold(second_taps, cotangent, text_embeds)
    w_out = g_out.whole
    g_self.step()
    second_out = product_back(second_taps, w_out)
    second_out, cotangent, text_embeds = ring.hold(second_out, cotangent, text_embeds)
    g_self.step()
    resnet = (masked + own_sum(second_out)) * keep
    resnet, cotangent, text_embeds = ring.hold(resnet, cotangent, text_embeds)
    g_self.step()

    attend_in, normal_self, scaling_self = norm_rows(resnet, gain_self_f)
    attend_all = flat(gather_rows(attend_in))
    g_text.begin()
    attend_all, cotangent = ring.hold(attend_all, cotangent)
    g_self.step()
    out_grad = cotangent.astype(f32) * keep
    feed_branch = flat(gather_rows(out_grad.astype(bf16)))
    w_self = g_self.whole
    qkv_full = w_self[:, : 3 * own_channels]
    cq_full = w_self[:, 3 * own_channels : 4 * own_channels]
    so_full = w_self[:, 4 * own_channels : 5 * own_channels]
    co_full = w_self[:, 5 * own_channels :]
    g_text.step()
    qkv = product(attend_all, qkv_full).astype(bf16)
    qkv = rows3(ring.hold(qkv))
    g_text.step()
    query_rows, key_rows, value_rows = jnp.split(qkv, 3, axis=2)
    mixture, self_chances = attend(query_rows, key_rows, value_rows, key_valid)
    self_part = product_back(flat(mixture), so_full)
    self_part = ring.hold(self_part)
    g_text.step()
    g_feed.begin()
    g_text.step()
    w_text = g_text.whole
    after_self = resnet + own_sum(self_part)
    g_feed.step()

    text_rows = flat(text_embeds)
    text_pair = product(text_rows, w_text).astype(bf16).reshape(slot_count, -1, 2 * own_channels)
    text_keys, text_values = jnp.split(text_pair, 2, axis=2)
    cross_in, normal_cross, scaling_cross = norm_rows(after_self, gain_cross_f)
    cross_all = flat(gather_rows(cross_in))
    cross_all = ring.hold(cross_all)
    g_feed.step()
    cross_rows = rows3(product(cross_all, cq_full).astype(bf16))
    cross_mix, cross_chances = attend(cross_rows, text_keys, text_values, None)
    cross_part = product_back(flat(cross_mix), co_full)
    cross_part = ring.hold(cross_part)
    g_feed.step()
    after_cross = after_self + own_sum(cross_part)

    feed_in, normal_feed, scaling_feed = norm_rows(after_cross, gain_feed_f)
    feed_in = ring.hold(feed_in)
    g_down.begin()
    g_feed.step()
    feed_all = flat(gather_rows(feed_in))
    w_feed = g_feed.whole
    g_down.step()
    pair_part = product(feed_all, w_feed)
    pair_part = ring.hold(pair_part)
    g_down.step()
    value_part, gate_part = pair_part[:, :hidden_own], pair_part[:, hidden_own:]
    lower = 0.5 * lax.erfc(-gate_part * math.sqrt(0.5))
    gelu_gate = gate_part * lower
    gelu_slope = lower + gate_part * jnp.exp(-0.5 * gate_part * gate_part) / math.sqrt(2 * math.pi)
    hidden = (value_part * gelu_gate).astype(bf16)
    hidden = ring.hold(hidden)
    g_down.step()
    s_down = Scattered(ring, weight_grad(feed_branch, hidden))
    g_down.step()
    w_down = g_down.whole

    s_down.step()
    hidden_grad = product(feed_branch, w_down)
    pair_grad = jnp.concatenate(
        [
            (hidden_grad * gelu_gate).astype(bf16),
            (hidden_grad * value_part * gelu_slope).astype(bf16),
        ],
        axis=1,
    )
    pair_grad = ring.hold(pair_grad)
    s_down.step()
    feed_part = product_back(pair_grad, w_feed)
    feed_part = ring.hold(feed_part)
    s_down.step()
    s_feed = Scattered(ring, weight_grad(feed_all, pair_grad))
    feed_back = own_sum(feed_part)
    feed_back = ring.hold(feed_back)
    s_down.step()
    feed_dv, grad_gain_feed = norm_rows_back(feed_back, normal_feed, scaling_feed, gain_feed_f)
    cross_grad = out_grad + feed_dv
    cross_branch = flat(gather_rows(cross_grad.astype(bf16)))
    cross_branch = ring.hold(cross_branch)
    s_feed.step()

    cross_mix_grad = rows3(product(cross_branch, co_full).astype(bf16))
    cross_dq, cross_dk, cross_dv = attend_back(
        cross_rows, text_keys, text_values, cross_mix_grad, cross_chances
    )
    cross_dq = flat(cross_dq)
    cross_dq, cross_dk, cross_dv = ring.hold(cross_dq, cross_dk, cross_dv)
    s_feed.step()
    cross_near = sum_near(product_back(cross_dq, cq_full), slot_count)
    cross_near = ring.hold(cross_near)
    s_feed.step()
    cross_back = sum_far(cross_near)
    grad_cross_out = weight_grad(cross_branch, flat(cross_mix))
    grad_cross_query = weight_grad(cross_all, cross_dq)
    s_cross = Scattered(
        ring,
        weight_grad(text_rows, flat(jnp.concatenate([cross_dk, cross_dv], axis=2))),
        jnp.concatenate([grad_cross_query, grad_cross_out], axis=1),
    )
    cross_dv_rows, grad_gain_cross = norm_rows_back(
        cross_back, normal_cross, scaling_cross, gain_cross_f
    )
    self_grad = cross_grad + cross_dv_rows

    self_branch = flat(gather_rows(self_grad.astype(bf16)))
    self_branch = ring.hold(self_branch)
    s_feed.step()
    mixture_grad = rows3(product(self_branch, so_full).astype(bf16))
    qkv_grad = flat(
        jnp.concatenate(
            attend_back(query_rows, key_rows, value_rows, mixture_grad, self_chances), axis=2
        )
    )
    qkv_grad = ring.hold(qkv_grad)
    s_cross.step()
    self_near = sum_near(product_back(qkv_grad, qkv_full), slot_count)
    self_near = ring.hold(self_near)
    s_cross.step()
    self_back = sum_far(self_near)
    self_dv_rows, grad_gain_self = norm_rows_back(self_back, normal_self, scaling_self, gain_self_f)
    resnet_grad = (self_grad + self_dv_rows) * keep
    resnet_branch = flat(gather_rows(resnet_grad.astype(bf16)))
    resnet_branch = ring.hold(resnet_branch)
    s_cross.step()

    second_parts = product(resnet_branch, w_out).astype(bf16)
    second_parts = ring.hold(second_parts)
    s_cross.step()
    grad_self_out = weight_grad(self_branch, flat(mixture))
    s_self = Scattered(
        ring, jnp.concatenate([weight_grad(attend_all, qkv_grad), grad_self_out], axis=1)
    )
    second_grad = shift_sum_back(tall, second_parts)
    second_grad = ring.hold(second_grad)
    s_self.step()
    s_out = Scattered(ring, weight_grad(resnet_branch, second_taps))
    mid_slope = silu_back(standard_mid * gain_mid_own, second_grad * keep_all)
    mid_gain_part = jnp.sum(mid_slope * standard_mid, axis=(0, 1))
    hat_mid = mid_slope * gain_mid_own
    mid_a = spread(group_sum(hat_mid, per_group) / counts[:, None], per_group)
    mid_b = spread(group_sum(hat_mid * standard_mid, per_group) / counts[:, None], per_group)
    middle_grad = (
        scaling_mid * (hat_mid - (mid_a + standard_mid * mid_b)) * keep_all
    ).astype(bf16)
    middle_grad = ring.hold(middle_grad)
    s_self.step()
    middle_taps = shift_stack_back(wide, flat(middle_grad))
    middle_taps = ring.hold(middle_taps)
    s_self.step()
    first_near = sum_near(product_back(middle_taps, w_in), slot_count)
    first_near = ring.hold(first_near)
    s_self.step()
    s_in = Scattered(ring, weight_grad(first_all, middle_taps))
    first_grad = sum_far(first_near)
    first_grad, hidden, middle_grad = ring.hold(first_grad, hidden, middle_grad)
    s_out.step()

    in_slope = silu_back(standard_in * gain_in_f, first_grad * keep)
    in_gain_part = jnp.sum(in_slope * standard_in, axis=(0, 1))
    hat_in = in_slope * gain_in_f
    in_a, in_b = lax.psum(
        (group_sum(hat_in, per_group), group_sum(hat_in * standard_in, per_group)), "mp"
    )
    in_a, in_b, in_gain_part, middle_grad, hidden = ring.hold(
        in_a, in_b, in_gain_part, middle_grad, hidden
    )
    s_out.step()
    in_a = spread(in_a / counts[:, None], per_group)
    in_b = spread(in_b / counts[:, None], per_group)
    grouped_grad = scaling_in * (hat_in - (in_a + standard_in * in_b))
    latent_grad = ((resnet_grad + grouped_grad) * keep).astype(bf16)

    time_sum = jnp.sum(middle_grad.astype(f32), axis=1)
    time_sum_all = share_small(time_sum, "dp").reshape(-1, own_channels)
    grad_time = jnp.einsum(
        "sa,sb->ab",
        time_act.astype(f32),
        time_sum_all,
        precision=highest,
        preferred_element_type=f32,
    )
    latent_grad, grad_time, in_gain_part, hidden = ring.hold(
        latent_grad, grad_time, in_gain_part, hidden
    )
    s_out.step()

    mid_gain_whole = lax.dynamic_update_slice_in_dim(
        jnp.zeros((channels,), f32), mid_gain_part, channel_start, 0
    )
    gain_parts = jnp.stack(
        [in_gain_part, mid_gain_whole, grad_gain_self, grad_gain_cross, grad_gain_feed]
    )
    gain_parts = jnp.swapaxes(gain_parts.reshape(5, dp_size, share), 0, 1)
    gain_parts = jnp.broadcast_to(gain_parts[:, None], (dp_size, mp_size, 5, share))
    gain_sums = lax.all_to_all(
        gain_parts.reshape(dp_size * mp_size, 5, share), ("dp", "mp"), 0, 0, tiled=True
    ).sum(0)
    gain_sums, hidden = ring.hold(gain_sums, hidden)
    s_out.step()
    output_near = sum_near(product_back(hidden, w_down), slot_count)
    output_near = ring.hold(output_near)
    s_in.step()
    output = ((after_cross + sum_far(output_near)) * keep).astype(bf16)
    output = ring.hold(output)
    s_in.step()
    s_in.step()
    s_in.step()
    sum_in, sum_out, sum_self = s_in.part, s_out.part, s_self.part
    sum_feed, sum_down = s_feed.part, s_down.part
    text_share = cross_key.shape[0]
    sum_text, sum_cross = s_cross.part[:text_share], s_cross.part[text_share:]

    def tap_part(values, tap):
        return values[:, tap * own_channels : (tap + 1) * own_channels]

    def column_part(values, part):
        return values[:, part * own_channels : (part + 1) * own_channels]

    return (
        output,
        latent_grad,
        jnp.stack([tap_part(sum_in, t) for t in range(TAPS)]).reshape(conv_in.shape),
        jnp.stack([tap_part(sum_out, t).T for t in range(TAPS)]).reshape(conv_out.shape),
        grad_time,
        column_part(sum_self, 0),
        column_part(sum_self, 1),
        column_part(sum_self, 2),
        column_part(sum_self, 3).T,
        column_part(sum_cross, 0),
        column_part(sum_text, 0),
        column_part(sum_text, 1),
        column_part(sum_cross, 1).T,
        sum_feed[:, :hidden_own],
        sum_feed[:, hidden_own:],
        sum_down.T,
        gain_sums[0],
        gain_sums[1],
        gain_sums[2],
        gain_sums[3],
        gain_sums[4],
    )


def solution(mesh):
    in_specs = (
        P("dp", "mp", None),
        P("dp", None, None),
        P("dp", "mp", None),
        P("dp"),
        P("dp"),
        P("dp"),
        P(None, None, "dp", "mp"),
        P(None, None, "mp", "dp"),
        P("dp", "mp"),
        P("dp", "mp"),
        P("dp", "mp"),
        P("dp", "mp"),
        P("mp", "dp"),
        P("dp", "mp"),
        P("dp", "mp"),
        P("dp", "mp"),
        P("mp", "dp"),
        P("dp", "mp"),
        P("dp", "mp"),
        P("mp", "dp"),
        P("dp"),
        P("dp"),
        P("dp"),
        P("dp"),
        P("dp"),
    )
    out_specs = (
        P("dp", "mp", None),
        P("dp", "mp", None),
        P(None, None, "dp", "mp"),
        P(None, None, "mp", "dp"),
        P("dp", "mp"),
        P("dp", "mp"),
        P("dp", "mp"),
        P("dp", "mp"),
        P("mp", "dp"),
        P("dp", "mp"),
        P("dp", "mp"),
        P("dp", "mp"),
        P("mp", "dp"),
        P("dp", "mp"),
        P("dp", "mp"),
        P("mp", "dp"),
        P("dp"),
        P("dp"),
        P("dp"),
        P("dp"),
        P("dp"),
    )
    return jax.shard_map(body, mesh=mesh, in_specs=in_specs, out_specs=out_specs, check_vma=False)
```

```python
import math

import jax
import jax.numpy as jnp
from jax import lax
from jax.experimental.layout import Layout, with_layout_constraint
from jax.sharding import PartitionSpec as P

C = 1280
HEAD_DIM = 64
GN_GROUPS = 32
SIDE = 16
TAPS = 9

highest = lax.Precision.HIGHEST
f32 = jnp.float32
bf16 = jnp.bfloat16


def ring_order(size):
    return list(range(0, size, 2)) + list(range(size - 1, 0, -2))


def ring_pairs(size):
    order = ring_order(size)
    right = [(order[i], order[(i + 1) % size]) for i in range(size)]
    return right, [(b, a) for a, b in right]


def ring_owners(size):
    order = ring_order(size)
    table = [[order[(order.index(i) + away) % size] for away in range(size)] for i in range(size)]
    row = lax.dynamic_slice(
        jnp.array(table, jnp.uint32),
        (lax.axis_index("dp").astype(jnp.uint32), jnp.uint32(0)),
        (1, size),
    )
    return [jnp.minimum(row[0, away], jnp.uint32(size - 1)) for away in range(size)]


class Gathered:
    def __init__(self, ring, pack, *parts):
        self.ring, self.pack, self.parts, self.taken = ring, pack, parts, 0

    def put(self, part, away, start):
        place = (self.ring.owner(away), jnp.uint32(start), jnp.uint32(0))
        self.whole = lax.dynamic_update_slice(self.whole, part[None], place)

    def begin(self):
        ring = self.ring
        if not ring.whole:
            self.whole = lax.all_gather(self.pack(*self.parts), "dp", axis=0, tiled=True)
            return
        zero = jnp.zeros((), self.parts[0].dtype)
        parts = self.parts
        if ring.last:
            zero, *parts = ring.hold(zero, *parts)
        self.block = self.pack(*parts)
        self.whole = jnp.broadcast_to(zero, (ring.size,) + self.block.shape)
        self.put(self.block, 0, 0)
        self.from_left = self.from_right = self.block

    def step(self):
        ring = self.ring
        if not ring.whole:
            return
        self.taken += 1
        size = ring.size
        rows, columns = self.block.shape
        if self.taken < size // 2:
            self.from_left, self.from_right = ring.step(self.from_left, self.from_right)
            self.put(self.from_left, size - self.taken, 0)
            self.put(self.from_right, self.taken, 0)
        else:
            half = rows // 2
            first, second = ring.step(self.from_left[:half], self.from_right[half:])
            self.put(first, size // 2, 0)
            self.put(second, size // 2, half)
            self.whole = self.whole.reshape(size * rows, columns)


class Scattered:
    def __init__(self, ring, *grads):
        self.ring, self.taken = ring, 0
        if not ring.whole:
            parts = [lax.psum_scatter(g, "dp", scatter_dimension=0, tiled=True) for g in grads]
            self.part = jnp.concatenate(parts).astype(f32)
            return
        self.blocks = [g.reshape(ring.size, -1, g.shape[1]) for g in grads]

    def own(self, away):
        place = self.ring.owner(away)
        zero = jnp.uint32(0)
        return jnp.concatenate(
            [
                lax.dynamic_slice(b, (place, zero, zero), (1,) + b.shape[1:])[0]
                for b in self.blocks
            ]
        )

    def step(self):
        ring = self.ring
        if not ring.whole:
            return
        size = ring.size
        half = sum(b.shape[1] for b in self.blocks) // 2
        away = size // 2 - self.taken
        self.taken += 1
        ahead, behind = self.own(away), self.own(size - away)
        if self.taken == 1:
            ahead, behind = ahead[:half], behind[half:]
        elif self.taken == 2:
            ahead = jnp.concatenate(
                [(ahead[:half].astype(f32) + self.from_left).astype(bf16), ahead[half:]]
            )
            behind = jnp.concatenate(
                [behind[:half], (behind[half:].astype(f32) + self.from_right).astype(bf16)]
            )
        else:
            ahead = (ahead.astype(f32) + self.from_left).astype(bf16)
            behind = (behind.astype(f32) + self.from_right).astype(bf16)
        self.from_left, self.from_right = ring.step(by_rows(ahead), by_rows(behind))
        if away == 1:
            self.part = (
                self.own(0).astype(f32)
                + self.from_left.astype(f32)
                + self.from_right.astype(f32)
            )


class Ring:
    def __init__(self):
        self.size = lax.axis_size("dp")
        self.whole = self.size == 8
        self.last = ()
        if self.whole:
            self.right, self.left = ring_pairs(self.size)
            self.owners = ring_owners(self.size)

    def step(self, to_right, to_left):
        if self.last:
            to_right, to_left = lax.optimization_barrier((to_right, to_left, self.last))[:2]
        self.last = (
            lax.ppermute(to_right, "dp", self.right),
            lax.ppermute(to_left, "dp", self.left),
        )
        return self.last

    def hold(self, *values):
        held = lax.optimization_barrier((values, self.last))[0]
        return held[0] if len(values) == 1 else held

    def owner(self, away):
        return self.owners[away % self.size]


def share_small(values, axis):
    size = lax.axis_size(axis)
    return lax.all_to_all(
        jnp.broadcast_to(values[None], (size,) + values.shape), axis, 0, 0, tiled=True
    )


def mp_bits():
    me = lax.axis_index("mp").astype(jnp.uint32)
    return me & 1, me >> 1


NEAR = [(0, 1), (1, 0), (2, 3), (3, 2)]
FAR = [(0, 2), (2, 0), (1, 3), (3, 1)]


def gather_rows(values):
    near_bit, far_bit = mp_bits()
    far = lax.ppermute(values, "mp", FAR)
    near = lax.ppermute(values, "mp", NEAR)
    both = lax.ppermute(far, "mp", NEAR)

    def pair(mine, other, bit):
        return jnp.concatenate(
            [jnp.where(bit == 0, mine, other), jnp.where(bit == 0, other, mine)], axis=1
        )

    return pair(pair(values, near, near_bit), pair(far, both, near_bit), far_bit)


def sum_near(values, items):
    near_bit, _ = mp_bits()
    parts = values.reshape(items, 2, 2, -1, values.shape[-1])

    def near_part(bit):
        zero = jnp.uint32(0)
        sizes = parts.shape[:2] + (1,) + parts.shape[3:]
        return lax.dynamic_slice(parts, (zero, zero, bit, zero, zero), sizes)[:, :, 0]

    got = lax.ppermute(near_part(1 - near_bit).astype(bf16), "mp", NEAR)
    return near_part(near_bit).astype(f32) + got.astype(f32)


def sum_far(held):
    _, far_bit = mp_bits()

    def far_part(bit):
        zero = jnp.uint32(0)
        sizes = held.shape[:1] + (1,) + held.shape[2:]
        return lax.dynamic_slice(held, (zero, bit, zero, zero), sizes)[:, 0]

    got = lax.ppermute(far_part(1 - far_bit).astype(bf16), "mp", FAR)
    return far_part(far_bit) + got.astype(f32)


def by_rows(values):
    return with_layout_constraint(values, Layout(major_to_minor=tuple(range(values.ndim))))


def flat(values):
    return values.reshape(-1, values.shape[-1])


def product(former, latter):
    return jnp.dot(former, latter, preferred_element_type=f32)


def product_back(former, latter):
    return lax.dot_general(former, latter, (((1,), (1,)), ((), ())), preferred_element_type=f32)


def product_down(former, latter):
    return lax.dot_general(former, latter, (((0,), (0,)), ((), ())), preferred_element_type=f32)


def weight_grad(former, latter):
    return by_rows(product_down(former, latter).astype(bf16))


def tap_sources(widths, item_rows):
    row = jnp.arange(item_rows, dtype=jnp.int32)
    step = jnp.arange(TAPS, dtype=jnp.int32)
    row_step, column_step = step // 3 - 1, step % 3 - 1
    column = row[None, :] % widths[:, None]
    beside = column[:, None, :] + column_step[None, :, None]
    usable = (beside >= 0) & (beside < widths[:, None, None])
    source = (
        row[None, None, :]
        + row_step[None, :, None] * widths[:, None, None]
        + column_step[None, :, None]
    )
    return jnp.where(usable, source, -1)


def tap_matrices(widths, item_rows):
    source = tap_sources(widths, item_rows)
    row = jnp.arange(item_rows, dtype=jnp.int32)
    tall = (source[:, :, :, None] == row).astype(bf16)
    tall = [by_rows(one.reshape(TAPS * item_rows, item_rows)) for one in tall]
    by_row = jnp.swapaxes(source, 1, 2)
    wide = (by_row[:, :, :, None] == row).astype(bf16)
    wide = [by_rows(one.reshape(item_rows, TAPS * item_rows)) for one in wide]
    return tall, wide


def items_of(values, count):
    rows = values.shape[0] // count
    return [values[i * rows : (i + 1) * rows] for i in range(count)]


def beside(stacked):
    rows = stacked.shape[0] // TAPS
    return jnp.concatenate([stacked[t * rows : (t + 1) * rows] for t in range(TAPS)], axis=1)


def below(values):
    columns = values.shape[1] // TAPS
    return jnp.concatenate(
        [values[:, t * columns : (t + 1) * columns] for t in range(TAPS)], axis=0
    )


def shift_stack(tall, values):
    return by_rows(
        jnp.concatenate(
            [
                beside(product(tap, item).astype(bf16))
                for tap, item in zip(tall, items_of(values, len(tall)))
            ]
        )
    )


def shift_stack_back(wide, values):
    return by_rows(
        jnp.concatenate(
            [
                beside(product_down(tap, item).astype(bf16))
                for tap, item in zip(wide, items_of(values, len(wide)))
            ]
        )
    )


def shift_sum(wide, values):
    return jnp.stack(
        [product(tap, below(item)) for tap, item in zip(wide, items_of(values, len(wide)))]
    )


def shift_sum_back(tall, values):
    return jnp.stack(
        [product_down(tap, below(item)) for tap, item in zip(tall, items_of(values, len(tall)))]
    )


def norm_rows(hidden, factor):
    center = hidden - jnp.mean(hidden, axis=-1, keepdims=True)
    scaling = lax.rsqrt(jnp.mean(center * center, axis=-1, keepdims=True) + 1e-05)
    normal = center * scaling
    return ((normal * factor).astype(bf16), normal, scaling)


def norm_rows_back(gradient, normal, scaling, factor):
    scaled = gradient * factor
    offset = jnp.mean(scaled, axis=-1, keepdims=True)
    slopes = jnp.mean(scaled * normal, axis=-1, keepdims=True)
    return (scaling * (scaled - offset - normal * slopes), jnp.sum(gradient * normal, axis=(0, 1)))


def group_sum(values, per_group):
    rows_summed = jnp.sum(values, axis=1)
    return rows_summed.reshape(values.shape[0], values.shape[2] // per_group, per_group).sum(-1)


def spread(values, per_group):
    return jnp.repeat(values, per_group, axis=-1)[:, None, :]


def silu_back(scaled, gradient):
    share = jax.nn.sigmoid(scaled)
    return gradient * share * (1.0 + scaled * (1.0 - share))


def split_heads(values):
    return values.reshape(values.shape[0], values.shape[1], values.shape[2] // HEAD_DIM, HEAD_DIM)


def attend(query_rows, key_rows, value_rows, key_valid):
    scores = jnp.einsum(
        "sqhd,skhd->shqk",
        split_heads(query_rows),
        split_heads(key_rows),
        preferred_element_type=f32,
    ) * HEAD_DIM ** (-0.5)
    if key_valid is not None:
        scores = jnp.where(key_valid[:, None, None, :], scores, -1e30)
    exponent = jnp.exp(scores - jnp.max(scores, axis=-1, keepdims=True))
    chances = exponent / jnp.sum(exponent, axis=-1, keepdims=True)
    mixture = jnp.einsum(
        "shqk,skhd->sqhd",
        chances.astype(bf16),
        split_heads(value_rows),
        preferred_element_type=f32,
    )
    return mixture.reshape(query_rows.shape).astype(bf16), chances


def attend_back(query_rows, key_rows, value_rows, mixture_grad, chances):
    query_heads = split_heads(query_rows)
    key_heads = split_heads(key_rows)
    value_heads = split_heads(value_rows)
    grad_heads = split_heads(mixture_grad)
    value_grad = jnp.einsum(
        "shqk,sqhd->skhd", chances.astype(bf16), grad_heads, preferred_element_type=f32
    )
    share_grad = jnp.einsum(
        "sqhd,skhd->shqk", grad_heads, value_heads, preferred_element_type=f32
    )
    inner_sum = jnp.sum(chances * share_grad, axis=-1, keepdims=True)
    score_grad = (chances * (share_grad - inner_sum)).astype(bf16)
    query_grad = jnp.einsum(
        "shqk,skhd->sqhd", score_grad, key_heads, preferred_element_type=f32
    ) * HEAD_DIM ** (-0.5)
    key_grad = jnp.einsum(
        "shqk,sqhd->skhd", score_grad, query_heads, preferred_element_type=f32
    ) * HEAD_DIM ** (-0.5)
    return (
        query_grad.reshape(query_rows.shape).astype(bf16),
        key_grad.reshape(key_rows.shape).astype(bf16),
        value_grad.reshape(value_rows.shape).astype(bf16),
    )


def body(
    latent,
    text_embeds,
    cotangent,
    item_count,
    bucket,
    timestep,
    conv_in,
    conv_out,
    time_weight,
    self_query,
    self_key,
    self_value,
    self_out,
    cross_query,
    cross_key,
    cross_value,
    cross_out,
    ff_value,
    ff_gate,
    ff_down,
    gn_in_gain,
    gn_mid_gain,
    self_gain,
    cross_gain,
    ff_gain,
):
    slot_count, local_rows, channels = latent.shape
    dp_size, mp_size = lax.axis_size("dp"), lax.axis_size("mp")
    item_rows = local_rows * mp_size
    per_group = channels // GN_GROUPS
    own_channels = conv_in.shape[3]
    share = conv_in.shape[2]
    dp_index, mp_index = lax.axis_index("dp"), lax.axis_index("mp")
    ring = Ring()

    def across(*parts):
        return jnp.concatenate(parts, axis=1)

    g_in = Gathered(ring, lambda k: across(*[k[t // 3, t % 3] for t in range(TAPS)]), conv_in)
    g_out = Gathered(ring, lambda k: across(*[k[t // 3, t % 3].T for t in range(TAPS)]), conv_out)
    g_self = Gathered(
        ring,
        lambda q, k, v, c, s, o: across(q, k, v, c, s.T, o.T),
        self_query,
        self_key,
        self_value,
        cross_query,
        self_out,
        cross_out,
    )
    g_text = Gathered(ring, across, cross_key, cross_value)
    g_feed = Gathered(ring, across, ff_value, ff_gate)
    g_down = Gathered(ring, lambda down: down.T, ff_down)
    hidden_own = ff_down.shape[0]

    g_in.begin()
    g_out.begin()
    g_in.step()
    gain_parts = jnp.stack([gn_in_gain, gn_mid_gain, self_gain, cross_gain, ff_gain]).astype(f32)
    small = jnp.concatenate([gain_parts.reshape(-1), timestep.astype(f32)])
    small_all = share_small(small, "dp")
    latent, item_count, bucket, later = ring.hold(
        latent, item_count, bucket, (cotangent, text_embeds)
    )
    g_in.step()

    is_live = (jnp.arange(slot_count, dtype=jnp.int32) < item_count[0]).astype(f32)
    widths = jnp.where(
        bucket == 0, SIDE, jnp.where(bucket == 1, 5 * SIDE // 4, 3 * SIDE // 2)
    ).astype(jnp.int32)
    heights = jnp.where(
        bucket == 0, SIDE, jnp.where(bucket == 1, 3 * SIDE // 4, 5 * SIDE // 8)
    ).astype(jnp.int32)
    filled = widths * heights
    position = mp_index * local_rows + jnp.arange(local_rows, dtype=jnp.int32)
    row_mask = (position[None, :] < filled[:, None]).astype(f32) * is_live[:, None]
    key_valid = jnp.arange(item_rows, dtype=jnp.int32)[None, :] < filled[:, None]
    full_mask = key_valid.astype(f32) * is_live[:, None]
    keep = row_mask[:, :, None]
    keep_all = full_mask[:, :, None]
    counts = filled.astype(f32) * per_group
    channel_start = mp_index * own_channels

    def rows3(values):
        return values.reshape(slot_count, item_rows, values.shape[-1])

    def own_sum(values):
        return sum_far(sum_near(values, slot_count))

    masked = latent.astype(f32) * keep
    all_positions = jnp.arange(item_rows, dtype=jnp.int32).reshape(mp_size, 1, local_rows)
    held = (all_positions < filled[None, :, None]).astype(f32).sum(-1) * is_live * per_group
    held_here = jnp.sum(row_mask, axis=1) * per_group
    local_sum = group_sum(masked, per_group)
    local_mean = local_sum / jnp.maximum(held_here, 1.0)[:, None]
    local_center = (masked - spread(local_mean, per_group)) * keep
    local_spread = group_sum(local_center * local_center, per_group)
    stats = share_small(jnp.stack([local_sum, local_spread]), "mp").reshape(
        mp_size, 2, slot_count, GN_GROUPS
    )
    stats, small_all, later = ring.hold(stats, small_all, later)
    g_in.step()
    gains = small_all[:, : 5 * share].reshape(dp_size, 5, share)
    gains = jnp.swapaxes(gains, 0, 1).reshape(5, channels)
    gain_in_f, gain_self_f, gain_cross_f, gain_feed_f = gains[0], gains[2], gains[3], gains[4]
    gain_mid_own = lax.dynamic_slice_in_dim(gains[1], channel_start, own_channels)
    steps_all = small_all[:, 5 * share :].reshape(-1)
    average = jnp.sum(stats[:, 0], axis=0) / counts[:, None]
    means = stats[:, 0] / jnp.maximum(held, 1.0)[:, :, None]
    variance = (
        jnp.sum(stats[:, 1] + held[:, :, None] * (means - average) ** 2, axis=0) / counts[:, None]
    )
    scaling_in = spread(lax.rsqrt(variance + 1e-06), per_group)
    standard_in = (masked - spread(average, per_group)) * scaling_in
    first_act = (jax.nn.silu(standard_in * gain_in_f) * keep).astype(bf16)
    first_all = flat(gather_rows(first_act))

    half_width = C // 2
    wave = dp_index * share + jnp.arange(share, dtype=jnp.int32)
    frequency = jnp.exp(-math.log(10000.0) * (wave % half_width).astype(f32) / half_width)
    angles = steps_all[:, None] * frequency[None, :]
    time_act = jax.nn.silu(
        jnp.where(wave[None, :] < half_width, jnp.cos(angles), jnp.sin(angles))
    ).astype(bf16)
    time_part = jnp.dot(time_act, time_weight, preferred_element_type=f32)
    first_all, time_part, later = ring.hold(first_all, time_part, later)
    g_in.step()
    first_all, time_part, shift_widths, later = ring.hold(first_all, time_part, widths, later)
    w_in = g_in.whole

    g_out.step()
    first_taps = product(first_all, w_in).astype(bf16)
    cotangent, text_embeds = later
    tall, wide = tap_matrices(shift_widths, item_rows)

    time_added = lax.all_to_all(
        time_part.reshape(dp_size, slot_count, own_channels), "dp", 0, 0, tiled=True
    ).sum(0)
    first_taps, time_added, cotangent, text_embeds = ring.hold(
        first_taps, time_added, cotangent, text_embeds
    )
    g_out.step()
    middle = (shift_sum(wide, first_taps) + time_added[:, None, :]) * keep_all
    middle, cotangent, text_embeds = ring.hold(middle, cotangent, text_embeds)
    g_out.step()
    average_mid = group_sum(middle, per_group) / counts[:, None]
    apart_mid = middle - spread(average_mid, per_group)
    center_mid = apart_mid * keep_all
    scaling_mid = spread(
        lax.rsqrt(group_sum(center_mid * center_mid, per_group) / counts[:, None] + 1e-06),
        per_group,
    )
    standard_mid = apart_mid * scaling_mid
    second_act = (jax.nn.silu(standard_mid * gain_mid_own) * keep_all).astype(bf16)
    second_act, cotangent, text_embeds = ring.hold(second_act, cotangent, text_embeds)
    g_self.begin()
    g_out.step()
    second_taps = shift_stack(tall, flat(second_act))
    second_taps, cotangent, text_embeds = ring.hold(second_taps, cotangent, text_embeds)
    w_out = g_out.whole
    g_self.step()
    second_out = product_back(second_taps, w_out)
    second_out, cotangent, text_embeds = ring.hold(second_out, cotangent, text_embeds)
    g_self.step()
    resnet = (masked + own_sum(second_out)) * keep
    resnet, cotangent, text_embeds = ring.hold(resnet, cotangent, text_embeds)
    g_self.step()

    attend_in, normal_self, scaling_self = norm_rows(resnet, gain_self_f)
    attend_all = flat(gather_rows(attend_in))
    g_text.begin()
    attend_all, cotangent = ring.hold(attend_all, cotangent)
    g_self.step()
    out_grad = cotangent.astype(f32) * keep
    feed_branch = flat(gather_rows(out_grad.astype(bf16)))
    w_self = g_self.whole
    qkv_full = w_self[:, : 3 * own_channels]
    cq_full = w_self[:, 3 * own_channels : 4 * own_channels]
    so_full = w_self[:, 4 * own_channels : 5 * own_channels]
    co_full = w_self[:, 5 * own_channels :]
    g_text.step()
    qkv = product(attend_all, qkv_full).astype(bf16)
    qkv = rows3(ring.hold(qkv))
    g_text.step()
    query_rows, key_rows, value_rows = jnp.split(qkv, 3, axis=2)
    mixture, self_chances = attend(query_rows, key_rows, value_rows, key_valid)
    self_part = product_back(flat(mixture), so_full)
    self_part = ring.hold(self_part)
    g_text.step()
    g_feed.begin()
    g_text.step()
    w_text = g_text.whole
    after_self = resnet + own_sum(self_part)
    g_feed.step()

    text_rows = flat(text_embeds)
    text_pair = product(text_rows, w_text).astype(bf16).reshape(slot_count, -1, 2 * own_channels)
    text_keys, text_values = jnp.split(text_pair, 2, axis=2)
    cross_in, normal_cross, scaling_cross = norm_rows(after_self, gain_cross_f)
    cross_all = flat(gather_rows(cross_in))
    cross_all = ring.hold(cross_all)
    g_feed.step()
    cross_rows = rows3(product(cross_all, cq_full).astype(bf16))
    cross_mix, cross_chances = attend(cross_rows, text_keys, text_values, None)
    cross_part = product_back(flat(cross_mix), co_full)
    cross_part = ring.hold(cross_part)
    g_feed.step()
    after_cross = after_self + own_sum(cross_part)

    feed_in, normal_feed, scaling_feed = norm_rows(after_cross, gain_feed_f)
    feed_in = ring.hold(feed_in)
    g_down.begin()
    g_feed.step()
    feed_all = flat(gather_rows(feed_in))
    w_feed = g_feed.whole
    g_down.step()
    pair_part = product(feed_all, w_feed)
    pair_part = ring.hold(pair_part)
    g_down.step()
    value_part, gate_part = pair_part[:, :hidden_own], pair_part[:, hidden_own:]
    lower = 0.5 * lax.erfc(-gate_part * math.sqrt(0.5))
    gelu_gate = gate_part * lower
    gelu_slope = lower + gate_part * jnp.exp(-0.5 * gate_part * gate_part) / math.sqrt(2 * math.pi)
    hidden = (value_part * gelu_gate).astype(bf16)
    hidden = ring.hold(hidden)
    g_down.step()
    s_down = Scattered(ring, weight_grad(feed_branch, hidden))
    g_down.step()
    w_down = g_down.whole

    s_down.step()
    hidden_grad = product(feed_branch, w_down)
    pair_grad = jnp.concatenate(
        [
            (hidden_grad * gelu_gate).astype(bf16),
            (hidden_grad * value_part * gelu_slope).astype(bf16),
        ],
        axis=1,
    )
    pair_grad = ring.hold(pair_grad)
    s_down.step()
    feed_part = product_back(pair_grad, w_feed)
    feed_part = ring.hold(feed_part)
    s_down.step()
    s_feed = Scattered(ring, weight_grad(feed_all, pair_grad))
    feed_back = own_sum(feed_part)
    feed_back = ring.hold(feed_back)
    s_down.step()
    feed_dv, grad_gain_feed = norm_rows_back(feed_back, normal_feed, scaling_feed, gain_feed_f)
    cross_grad = out_grad + feed_dv
    cross_branch = flat(gather_rows(cross_grad.astype(bf16)))
    cross_branch = ring.hold(cross_branch)
    s_feed.step()

    cross_mix_grad = rows3(product(cross_branch, co_full).astype(bf16))
    cross_dq, cross_dk, cross_dv = attend_back(
        cross_rows, text_keys, text_values, cross_mix_grad, cross_chances
    )
    cross_dq = flat(cross_dq)
    cross_dq, cross_dk, cross_dv = ring.hold(cross_dq, cross_dk, cross_dv)
    s_feed.step()
    cross_near = sum_near(product_back(cross_dq, cq_full), slot_count)
    cross_near = ring.hold(cross_near)
    s_feed.step()
    cross_back = sum_far(cross_near)
    grad_cross_out = weight_grad(cross_branch, flat(cross_mix))
    grad_cross_query = weight_grad(cross_all, cross_dq)
    s_cross = Scattered(
        ring,
        weight_grad(text_rows, flat(jnp.concatenate([cross_dk, cross_dv], axis=2))),
        jnp.concatenate([grad_cross_query, grad_cross_out], axis=1),
    )
    cross_dv_rows, grad_gain_cross = norm_rows_back(
        cross_back, normal_cross, scaling_cross, gain_cross_f
    )
    self_grad = cross_grad + cross_dv_rows

    self_branch = flat(gather_rows(self_grad.astype(bf16)))
    self_branch = ring.hold(self_branch)
    s_feed.step()
    mixture_grad = rows3(product(self_branch, so_full).astype(bf16))
    qkv_grad = flat(
        jnp.concatenate(
            attend_back(query_rows, key_rows, value_rows, mixture_grad, self_chances), axis=2
        )
    )
    qkv_grad = ring.hold(qkv_grad)
    s_cross.step()
    self_near = sum_near(product_back(qkv_grad, qkv_full), slot_count)
    self_near = ring.hold(self_near)
    s_cross.step()
    self_back = sum_far(self_near)
    self_dv_rows, grad_gain_self = norm_rows_back(self_back, normal_self, scaling_self, gain_self_f)
    resnet_grad = (self_grad + self_dv_rows) * keep
    resnet_branch = flat(gather_rows(resnet_grad.astype(bf16)))
    resnet_branch = ring.hold(resnet_branch)
    s_cross.step()

    second_parts = product(resnet_branch, w_out).astype(bf16)
    second_parts = ring.hold(second_parts)
    s_cross.step()
    grad_self_out = weight_grad(self_branch, flat(mixture))
    s_self = Scattered(
        ring, jnp.concatenate([weight_grad(attend_all, qkv_grad), grad_self_out], axis=1)
    )
    second_grad = shift_sum_back(tall, second_parts)
    second_grad = ring.hold(second_grad)
    s_self.step()
    s_out = Scattered(ring, weight_grad(resnet_branch, second_taps))
    mid_slope = silu_back(standard_mid * gain_mid_own, second_grad * keep_all)
    mid_gain_part = jnp.sum(mid_slope * standard_mid, axis=(0, 1))
    hat_mid = mid_slope * gain_mid_own
    mid_a = spread(group_sum(hat_mid, per_group) / counts[:, None], per_group)
    mid_b = spread(group_sum(hat_mid * standard_mid, per_group) / counts[:, None], per_group)
    middle_grad = (
        scaling_mid * (hat_mid - (mid_a + standard_mid * mid_b)) * keep_all
    ).astype(bf16)
    middle_grad = ring.hold(middle_grad)
    s_self.step()
    middle_taps = shift_stack_back(wide, flat(middle_grad))
    middle_taps = ring.hold(middle_taps)
    s_self.step()
    first_near = sum_near(product_back(middle_taps, w_in), slot_count)
    first_near = ring.hold(first_near)
    s_self.step()
    in_grad = weight_grad(first_all, middle_taps)
    cut = in_grad.shape[1] // 256 * 128
    s_in = Scattered(ring, in_grad[:, :cut])
    first_grad = sum_far(first_near)
    first_grad, hidden, middle_grad = ring.hold(first_grad, hidden, middle_grad)
    s_out.step()

    in_slope = silu_back(standard_in * gain_in_f, first_grad * keep)
    in_gain_part = jnp.sum(in_slope * standard_in, axis=(0, 1))
    hat_in = in_slope * gain_in_f
    in_a, in_b = lax.psum(
        (group_sum(hat_in, per_group), group_sum(hat_in * standard_in, per_group)), "mp"
    )
    in_a, in_b, in_gain_part, middle_grad, hidden = ring.hold(
        in_a, in_b, in_gain_part, middle_grad, hidden
    )
    s_out.step()
    in_a = spread(in_a / counts[:, None], per_group)
    in_b = spread(in_b / counts[:, None], per_group)
    grouped_grad = scaling_in * (hat_in - (in_a + standard_in * in_b))
    latent_grad = ((resnet_grad + grouped_grad) * keep).astype(bf16)

    latent_grad, in_gain_part, middle_grad, hidden = ring.hold(
        latent_grad, in_gain_part, middle_grad, hidden
    )
    s_out.step()
    s_out.step()
    in_gain_part, middle_grad, hidden = ring.hold(in_gain_part, middle_grad, hidden)
    other = Ring()
    other.last = ring.last
    s_rest = Scattered(other, in_grad[:, cut:])
    s_in.step()
    s_rest.step()

    mid_gain_whole = lax.dynamic_update_slice_in_dim(
        jnp.zeros((channels,), f32), mid_gain_part, channel_start, 0
    )
    gain_parts = jnp.stack(
        [in_gain_part, mid_gain_whole, grad_gain_self, grad_gain_cross, grad_gain_feed]
    )
    gain_parts = jnp.swapaxes(gain_parts.reshape(5, dp_size, share), 0, 1)
    gain_parts = jnp.broadcast_to(gain_parts[:, None], (dp_size, mp_size, 5, share))
    time_sum = jnp.sum(middle_grad.astype(f32), axis=1).reshape(1, -1)
    payload = jnp.concatenate(
        [
            gain_parts.reshape(dp_size * mp_size, 5 * share),
            jnp.broadcast_to(time_sum, (dp_size * mp_size, time_sum.shape[1])),
        ],
        axis=1,
    )
    payload = lax.all_to_all(payload, ("dp", "mp"), 0, 0, tiled=True)
    gain_sums = payload[:, : 5 * share].sum(0).reshape(5, share)
    time_sum_all = payload[:, 5 * share :].reshape(dp_size, mp_size, -1)
    time_sum_all = lax.dynamic_index_in_dim(time_sum_all, mp_index, 1, keepdims=False)
    grad_time = jnp.einsum(
        "sa,sb->ab",
        time_act.astype(f32),
        time_sum_all.reshape(-1, own_channels),
        precision=highest,
        preferred_element_type=f32,
    )
    gain_sums, grad_time, hidden = ring.hold(gain_sums, grad_time, hidden)
    s_in.step()
    s_rest.step()
    output_near = sum_near(product_back(hidden, w_down), slot_count)
    s_in.step()
    s_rest.step()
    output = ((after_cross + sum_far(output_near)) * keep).astype(bf16)
    s_in.step()
    s_rest.step()
    sum_in = jnp.concatenate([s_in.part, s_rest.part], axis=1)
    sum_out, sum_self = s_out.part, s_self.part
    sum_feed, sum_down = s_feed.part, s_down.part
    text_share = cross_key.shape[0]
    sum_text, sum_cross = s_cross.part[:text_share], s_cross.part[text_share:]

    def tap_part(values, tap):
        return values[:, tap * own_channels : (tap + 1) * own_channels]

    def column_part(values, part):
        return values[:, part * own_channels : (part + 1) * own_channels]

    return (
        output,
        latent_grad,
        jnp.stack([tap_part(sum_in, t) for t in range(TAPS)]).reshape(conv_in.shape),
        jnp.stack([tap_part(sum_out, t).T for t in range(TAPS)]).reshape(conv_out.shape),
        grad_time,
        column_part(sum_self, 0),
        column_part(sum_self, 1),
        column_part(sum_self, 2),
        column_part(sum_self, 3).T,
        column_part(sum_cross, 0),
        column_part(sum_text, 0),
        column_part(sum_text, 1),
        column_part(sum_cross, 1).T,
        sum_feed[:, :hidden_own],
        sum_feed[:, hidden_own:],
        sum_down.T,
        gain_sums[0],
        gain_sums[1],
        gain_sums[2],
        gain_sums[3],
        gain_sums[4],
    )


def solution(mesh):
    in_specs = (
        P("dp", "mp", None),
        P("dp", None, None),
        P("dp", "mp", None),
        P("dp"),
        P("dp"),
        P("dp"),
        P(None, None, "dp", "mp"),
        P(None, None, "mp", "dp"),
        P("dp", "mp"),
        P("dp", "mp"),
        P("dp", "mp"),
        P("dp", "mp"),
        P("mp", "dp"),
        P("dp", "mp"),
        P("dp", "mp"),
        P("dp", "mp"),
        P("mp", "dp"),
        P("dp", "mp"),
        P("dp", "mp"),
        P("mp", "dp"),
        P("dp"),
        P("dp"),
        P("dp"),
        P("dp"),
        P("dp"),
    )
    out_specs = (
        P("dp", "mp", None),
        P("dp", "mp", None),
        P(None, None, "dp", "mp"),
        P(None, None, "mp", "dp"),
        P("dp", "mp"),
        P("dp", "mp"),
        P("dp", "mp"),
        P("dp", "mp"),
        P("mp", "dp"),
        P("dp", "mp"),
        P("dp", "mp"),
        P("dp", "mp"),
        P("mp", "dp"),
        P("dp", "mp"),
        P("dp", "mp"),
        P("mp", "dp"),
        P("dp"),
        P("dp"),
        P("dp"),
        P("dp"),
        P("dp"),
    )
    return jax.shard_map(body, mesh=mesh, in_specs=in_specs, out_specs=out_specs, check_vma=False)
```

```python
import math

import jax
import jax.numpy as jnp
from jax import lax
from jax.experimental.layout import Layout, with_layout_constraint
from jax.sharding import PartitionSpec as P

C = 1280
HEAD_DIM = 64
GN_GROUPS = 32
SIDE = 16
TAPS = 9

highest = lax.Precision.HIGHEST
f32 = jnp.float32
bf16 = jnp.bfloat16


def ring_order(size):
    return list(range(0, size, 2)) + list(range(size - 1, 0, -2))


def ring_pairs(size):
    order = ring_order(size)
    right = [(order[i], order[(i + 1) % size]) for i in range(size)]
    return right, [(b, a) for a, b in right]


def ring_owners(size):
    order = ring_order(size)
    table = [[order[(order.index(i) + away) % size] for away in range(size)] for i in range(size)]
    row = lax.dynamic_slice(
        jnp.array(table, jnp.uint32),
        (lax.axis_index("dp").astype(jnp.uint32), jnp.uint32(0)),
        (1, size),
    )
    return [jnp.minimum(row[0, away], jnp.uint32(size - 1)) for away in range(size)]


class Gathered:
    def __init__(self, ring, pack, *parts):
        self.ring, self.pack, self.parts, self.taken = ring, pack, parts, 0

    def put(self, part, away, start):
        place = (self.ring.owner(away), jnp.uint32(start), jnp.uint32(0))
        self.whole = lax.dynamic_update_slice(self.whole, part[None], place)

    def begin(self):
        ring = self.ring
        if not ring.whole:
            self.whole = lax.all_gather(self.pack(*self.parts), "dp", axis=0, tiled=True)
            return
        zero = jnp.zeros((), self.parts[0].dtype)
        parts = self.parts
        if ring.last:
            zero, *parts = ring.hold(zero, *parts)
        self.block = self.pack(*parts)
        self.whole = jnp.broadcast_to(zero, (ring.size,) + self.block.shape)
        self.put(self.block, 0, 0)
        self.from_left = self.from_right = self.block

    def step(self):
        ring = self.ring
        if not ring.whole:
            return
        self.taken += 1
        size = ring.size
        rows, columns = self.block.shape
        if self.taken < size // 2:
            self.from_left, self.from_right = ring.step(self.from_left, self.from_right)
            self.put(self.from_left, size - self.taken, 0)
            self.put(self.from_right, self.taken, 0)
        else:
            half = rows // 2
            first, second = ring.step(self.from_left[:half], self.from_right[half:])
            self.put(first, size // 2, 0)
            self.put(second, size // 2, half)
            self.whole = self.whole.reshape(size * rows, columns)


class Scattered:
    def __init__(self, ring, *grads):
        self.ring, self.taken = ring, 0
        if not ring.whole:
            parts = [lax.psum_scatter(g, "dp", scatter_dimension=0, tiled=True) for g in grads]
            self.part = jnp.concatenate(parts).astype(f32)
            return
        self.blocks = [g.reshape(ring.size, -1, g.shape[1]) for g in grads]

    def own(self, away):
        place = self.ring.owner(away)
        zero = jnp.uint32(0)
        return jnp.concatenate(
            [
                lax.dynamic_slice(b, (place, zero, zero), (1,) + b.shape[1:])[0]
                for b in self.blocks
            ]
        )

    def step(self):
        ring = self.ring
        if not ring.whole:
            return
        size = ring.size
        half = sum(b.shape[1] for b in self.blocks) // 2
        away = size // 2 - self.taken
        self.taken += 1
        ahead, behind = self.own(away), self.own(size - away)
        if self.taken == 1:
            ahead, behind = ahead[:half], behind[half:]
        elif self.taken == 2:
            ahead = jnp.concatenate(
                [(ahead[:half].astype(f32) + self.from_left).astype(bf16), ahead[half:]]
            )
            behind = jnp.concatenate(
                [behind[:half], (behind[half:].astype(f32) + self.from_right).astype(bf16)]
            )
        else:
            ahead = (ahead.astype(f32) + self.from_left).astype(bf16)
            behind = (behind.astype(f32) + self.from_right).astype(bf16)
        self.from_left, self.from_right = ring.step(by_rows(ahead), by_rows(behind))
        if away == 1:
            self.part = (
                self.own(0).astype(f32)
                + self.from_left.astype(f32)
                + self.from_right.astype(f32)
            )


class Ring:
    def __init__(self):
        self.size = lax.axis_size("dp")
        self.whole = self.size == 8
        self.last = ()
        if self.whole:
            self.right, self.left = ring_pairs(self.size)
            self.owners = ring_owners(self.size)

    def step(self, to_right, to_left):
        if self.last:
            to_right, to_left = lax.optimization_barrier((to_right, to_left, self.last))[:2]
        self.last = (
            lax.ppermute(to_right, "dp", self.right),
            lax.ppermute(to_left, "dp", self.left),
        )
        return self.last

    def hold(self, *values):
        held = lax.optimization_barrier((values, self.last))[0]
        return held[0] if len(values) == 1 else held

    def owner(self, away):
        return self.owners[away % self.size]


def share_small(values, axis):
    size = lax.axis_size(axis)
    return lax.all_to_all(
        jnp.broadcast_to(values[None], (size,) + values.shape), axis, 0, 0, tiled=True
    )


def mp_bits():
    me = lax.axis_index("mp").astype(jnp.uint32)
    return me & 1, me >> 1


NEAR = [(0, 1), (1, 0), (2, 3), (3, 2)]
FAR = [(0, 2), (2, 0), (1, 3), (3, 1)]


def gather_rows(values):
    near_bit, far_bit = mp_bits()
    far = lax.ppermute(values, "mp", FAR)
    near = lax.ppermute(values, "mp", NEAR)
    both = lax.ppermute(far, "mp", NEAR)

    def pair(mine, other, bit):
        return jnp.concatenate(
            [jnp.where(bit == 0, mine, other), jnp.where(bit == 0, other, mine)], axis=1
        )

    return pair(pair(values, near, near_bit), pair(far, both, near_bit), far_bit)


def sum_near(values, items):
    near_bit, _ = mp_bits()
    parts = values.reshape(items, 2, 2, -1, values.shape[-1])

    def near_part(bit):
        zero = jnp.uint32(0)
        sizes = parts.shape[:2] + (1,) + parts.shape[3:]
        return lax.dynamic_slice(parts, (zero, zero, bit, zero, zero), sizes)[:, :, 0]

    got = lax.ppermute(near_part(1 - near_bit).astype(bf16), "mp", NEAR)
    return near_part(near_bit).astype(f32) + got.astype(f32)


def sum_far(held):
    _, far_bit = mp_bits()

    def far_part(bit):
        zero = jnp.uint32(0)
        sizes = held.shape[:1] + (1,) + held.shape[2:]
        return lax.dynamic_slice(held, (zero, bit, zero, zero), sizes)[:, 0]

    got = lax.ppermute(far_part(1 - far_bit).astype(bf16), "mp", FAR)
    return far_part(far_bit) + got.astype(f32)


def by_rows(values):
    return with_layout_constraint(values, Layout(major_to_minor=tuple(range(values.ndim))))


def flat(values):
    return values.reshape(-1, values.shape[-1])


def product(former, latter):
    return jnp.dot(former, latter, preferred_element_type=f32)


def product_back(former, latter):
    return lax.dot_general(former, latter, (((1,), (1,)), ((), ())), preferred_element_type=f32)


def product_down(former, latter):
    return lax.dot_general(former, latter, (((0,), (0,)), ((), ())), preferred_element_type=f32)


def weight_grad(former, latter):
    return by_rows(product_down(former, latter).astype(bf16))


def tap_sources(widths, item_rows):
    row = jnp.arange(item_rows, dtype=jnp.int32)
    step = jnp.arange(TAPS, dtype=jnp.int32)
    row_step, column_step = step // 3 - 1, step % 3 - 1
    column = row[None, :] % widths[:, None]
    beside = column[:, None, :] + column_step[None, :, None]
    usable = (beside >= 0) & (beside < widths[:, None, None])
    source = (
        row[None, None, :]
        + row_step[None, :, None] * widths[:, None, None]
        + column_step[None, :, None]
    )
    return jnp.where(usable, source, -1)


def tap_matrices(widths, item_rows):
    source = tap_sources(widths, item_rows)
    row = jnp.arange(item_rows, dtype=jnp.int32)
    tall = (source[:, :, :, None] == row).astype(bf16)
    tall = [by_rows(one.reshape(TAPS * item_rows, item_rows)) for one in tall]
    by_row = jnp.swapaxes(source, 1, 2)
    wide = (by_row[:, :, :, None] == row).astype(bf16)
    wide = [by_rows(one.reshape(item_rows, TAPS * item_rows)) for one in wide]
    return tall, wide


def items_of(values, count):
    rows = values.shape[0] // count
    return [values[i * rows : (i + 1) * rows] for i in range(count)]


def beside(stacked):
    rows = stacked.shape[0] // TAPS
    return jnp.concatenate([stacked[t * rows : (t + 1) * rows] for t in range(TAPS)], axis=1)


def below(values):
    columns = values.shape[1] // TAPS
    return jnp.concatenate(
        [values[:, t * columns : (t + 1) * columns] for t in range(TAPS)], axis=0
    )


def shift_stack(tall, values):
    return by_rows(
        jnp.concatenate(
            [
                beside(product(tap, item).astype(bf16))
                for tap, item in zip(tall, items_of(values, len(tall)))
            ]
        )
    )


def shift_stack_back(wide, values):
    return by_rows(
        jnp.concatenate(
            [
                beside(product_down(tap, item).astype(bf16))
                for tap, item in zip(wide, items_of(values, len(wide)))
            ]
        )
    )


def shift_sum(wide, values):
    return jnp.stack(
        [product(tap, below(item)) for tap, item in zip(wide, items_of(values, len(wide)))]
    )


def shift_sum_back(tall, values):
    return jnp.stack(
        [product_down(tap, below(item)) for tap, item in zip(tall, items_of(values, len(tall)))]
    )


def norm_rows(hidden, factor):
    center = hidden - jnp.mean(hidden, axis=-1, keepdims=True)
    scaling = lax.rsqrt(jnp.mean(center * center, axis=-1, keepdims=True) + 1e-05)
    normal = center * scaling
    return ((normal * factor).astype(bf16), normal, scaling)


def norm_rows_back(gradient, normal, scaling, factor):
    scaled = gradient * factor
    offset = jnp.mean(scaled, axis=-1, keepdims=True)
    slopes = jnp.mean(scaled * normal, axis=-1, keepdims=True)
    return (scaling * (scaled - offset - normal * slopes), jnp.sum(gradient * normal, axis=(0, 1)))


def group_sum(values, per_group):
    rows_summed = jnp.sum(values, axis=1)
    return rows_summed.reshape(values.shape[0], values.shape[2] // per_group, per_group).sum(-1)


def spread(values, per_group):
    return jnp.repeat(values, per_group, axis=-1)[:, None, :]


def silu_back(scaled, gradient):
    share = jax.nn.sigmoid(scaled)
    return gradient * share * (1.0 + scaled * (1.0 - share))


def split_heads(values):
    return values.reshape(values.shape[0], values.shape[1], values.shape[2] // HEAD_DIM, HEAD_DIM)


def attend(query_rows, key_rows, value_rows, key_valid):
    scores = jnp.einsum(
        "sqhd,skhd->shqk",
        split_heads(query_rows),
        split_heads(key_rows),
        preferred_element_type=f32,
    ) * HEAD_DIM ** (-0.5)
    if key_valid is not None:
        scores = jnp.where(key_valid[:, None, None, :], scores, -1e30)
    exponent = jnp.exp(scores - jnp.max(scores, axis=-1, keepdims=True))
    chances = exponent / jnp.sum(exponent, axis=-1, keepdims=True)
    mixture = jnp.einsum(
        "shqk,skhd->sqhd",
        chances.astype(bf16),
        split_heads(value_rows),
        preferred_element_type=f32,
    )
    return mixture.reshape(query_rows.shape).astype(bf16), chances


def attend_back(query_rows, key_rows, value_rows, mixture_grad, chances):
    query_heads = split_heads(query_rows)
    key_heads = split_heads(key_rows)
    value_heads = split_heads(value_rows)
    grad_heads = split_heads(mixture_grad)
    value_grad = jnp.einsum(
        "shqk,sqhd->skhd", chances.astype(bf16), grad_heads, preferred_element_type=f32
    )
    share_grad = jnp.einsum(
        "sqhd,skhd->shqk", grad_heads, value_heads, preferred_element_type=f32
    )
    inner_sum = jnp.sum(chances * share_grad, axis=-1, keepdims=True)
    score_grad = (chances * (share_grad - inner_sum)).astype(bf16)
    query_grad = jnp.einsum(
        "shqk,skhd->sqhd", score_grad, key_heads, preferred_element_type=f32
    ) * HEAD_DIM ** (-0.5)
    key_grad = jnp.einsum(
        "shqk,sqhd->skhd", score_grad, query_heads, preferred_element_type=f32
    ) * HEAD_DIM ** (-0.5)
    return (
        query_grad.reshape(query_rows.shape).astype(bf16),
        key_grad.reshape(key_rows.shape).astype(bf16),
        value_grad.reshape(value_rows.shape).astype(bf16),
    )


def body(
    latent,
    text_embeds,
    cotangent,
    item_count,
    bucket,
    timestep,
    conv_in,
    conv_out,
    time_weight,
    self_query,
    self_key,
    self_value,
    self_out,
    cross_query,
    cross_key,
    cross_value,
    cross_out,
    ff_value,
    ff_gate,
    ff_down,
    gn_in_gain,
    gn_mid_gain,
    self_gain,
    cross_gain,
    ff_gain,
):
    slot_count, local_rows, channels = latent.shape
    dp_size, mp_size = lax.axis_size("dp"), lax.axis_size("mp")
    item_rows = local_rows * mp_size
    per_group = channels // GN_GROUPS
    own_channels = conv_in.shape[3]
    share = conv_in.shape[2]
    dp_index, mp_index = lax.axis_index("dp"), lax.axis_index("mp")
    ring = Ring()

    def across(*parts):
        return jnp.concatenate(parts, axis=1)

    g_in = Gathered(ring, lambda k: across(*[k[t // 3, t % 3] for t in range(TAPS)]), conv_in)
    g_out = Gathered(ring, lambda k: across(*[k[t // 3, t % 3].T for t in range(TAPS)]), conv_out)
    g_self = Gathered(
        ring,
        lambda q, k, v, c, s, o: across(q, k, v, c, s.T, o.T),
        self_query,
        self_key,
        self_value,
        cross_query,
        self_out,
        cross_out,
    )
    g_text = Gathered(ring, across, cross_key, cross_value)
    g_feed = Gathered(ring, across, ff_value, ff_gate)
    g_down = Gathered(ring, lambda down: down.T, ff_down)
    hidden_own = ff_down.shape[0]

    g_in.begin()
    g_out.begin()
    g_in.step()
    gain_parts = jnp.stack([gn_in_gain, gn_mid_gain, self_gain, cross_gain, ff_gain]).astype(f32)
    small = jnp.concatenate([gain_parts.reshape(-1), timestep.astype(f32)])
    small_all = share_small(small, "dp")
    latent, item_count, bucket, later = ring.hold(
        latent, item_count, bucket, (cotangent, text_embeds)
    )
    g_in.step()

    is_live = (jnp.arange(slot_count, dtype=jnp.int32) < item_count[0]).astype(f32)
    widths = jnp.where(
        bucket == 0, SIDE, jnp.where(bucket == 1, 5 * SIDE // 4, 3 * SIDE // 2)
    ).astype(jnp.int32)
    heights = jnp.where(
        bucket == 0, SIDE, jnp.where(bucket == 1, 3 * SIDE // 4, 5 * SIDE // 8)
    ).astype(jnp.int32)
    filled = widths * heights
    position = mp_index * local_rows + jnp.arange(local_rows, dtype=jnp.int32)
    row_mask = (position[None, :] < filled[:, None]).astype(f32) * is_live[:, None]
    key_valid = jnp.arange(item_rows, dtype=jnp.int32)[None, :] < filled[:, None]
    full_mask = key_valid.astype(f32) * is_live[:, None]
    keep = row_mask[:, :, None]
    keep_all = full_mask[:, :, None]
    counts = filled.astype(f32) * per_group
    channel_start = mp_index * own_channels

    def rows3(values):
        return values.reshape(slot_count, item_rows, values.shape[-1])

    def own_sum(values):
        return sum_far(sum_near(values, slot_count))

    masked = latent.astype(f32) * keep
    all_positions = jnp.arange(item_rows, dtype=jnp.int32).reshape(mp_size, 1, local_rows)
    held = (all_positions < filled[None, :, None]).astype(f32).sum(-1) * is_live * per_group
    held_here = jnp.sum(row_mask, axis=1) * per_group
    local_sum = group_sum(masked, per_group)
    local_mean = local_sum / jnp.maximum(held_here, 1.0)[:, None]
    local_center = (masked - spread(local_mean, per_group)) * keep
    local_spread = group_sum(local_center * local_center, per_group)
    stats = share_small(jnp.stack([local_sum, local_spread]), "mp").reshape(
        mp_size, 2, slot_count, GN_GROUPS
    )
    stats, small_all, later = ring.hold(stats, small_all, later)
    g_in.step()
    gains = small_all[:, : 5 * share].reshape(dp_size, 5, share)
    gains = jnp.swapaxes(gains, 0, 1).reshape(5, channels)
    gain_in_f, gain_self_f, gain_cross_f, gain_feed_f = gains[0], gains[2], gains[3], gains[4]
    gain_mid_own = lax.dynamic_slice_in_dim(gains[1], channel_start, own_channels)
    steps_all = small_all[:, 5 * share :].reshape(-1)
    average = jnp.sum(stats[:, 0], axis=0) / counts[:, None]
    means = stats[:, 0] / jnp.maximum(held, 1.0)[:, :, None]
    variance = (
        jnp.sum(stats[:, 1] + held[:, :, None] * (means - average) ** 2, axis=0) / counts[:, None]
    )
    scaling_in = spread(lax.rsqrt(variance + 1e-06), per_group)
    standard_in = (masked - spread(average, per_group)) * scaling_in
    first_act = (jax.nn.silu(standard_in * gain_in_f) * keep).astype(bf16)
    first_all = flat(gather_rows(first_act))

    half_width = C // 2
    wave = dp_index * share + jnp.arange(share, dtype=jnp.int32)
    frequency = jnp.exp(-math.log(10000.0) * (wave % half_width).astype(f32) / half_width)
    angles = steps_all[:, None] * frequency[None, :]
    time_act = jax.nn.silu(
        jnp.where(wave[None, :] < half_width, jnp.cos(angles), jnp.sin(angles))
    ).astype(bf16)
    time_part = jnp.dot(time_act, time_weight, preferred_element_type=f32)
    first_all, time_part, later = ring.hold(first_all, time_part, later)
    g_in.step()
    first_all, time_part, shift_widths, later = ring.hold(first_all, time_part, widths, later)
    w_in = g_in.whole

    g_out.step()
    first_taps = product(first_all, w_in).astype(bf16)
    cotangent, text_embeds = later
    tall, wide = tap_matrices(shift_widths, item_rows)

    time_added = lax.all_to_all(
        time_part.reshape(dp_size, slot_count, own_channels), "dp", 0, 0, tiled=True
    ).sum(0)
    first_taps, time_added, cotangent, text_embeds = ring.hold(
        first_taps, time_added, cotangent, text_embeds
    )
    g_out.step()
    middle = (shift_sum(wide, first_taps) + time_added[:, None, :]) * keep_all
    middle, cotangent, text_embeds = ring.hold(middle, cotangent, text_embeds)
    g_out.step()
    average_mid = group_sum(middle, per_group) / counts[:, None]
    apart_mid = middle - spread(average_mid, per_group)
    center_mid = apart_mid * keep_all
    scaling_mid = spread(
        lax.rsqrt(group_sum(center_mid * center_mid, per_group) / counts[:, None] + 1e-06),
        per_group,
    )
    standard_mid = apart_mid * scaling_mid
    second_act = (jax.nn.silu(standard_mid * gain_mid_own) * keep_all).astype(bf16)
    second_act, cotangent, text_embeds = ring.hold(second_act, cotangent, text_embeds)
    g_self.begin()
    g_out.step()
    second_taps = shift_stack(tall, flat(second_act))
    second_taps, cotangent, text_embeds = ring.hold(second_taps, cotangent, text_embeds)
    w_out = g_out.whole
    g_self.step()
    second_out = product_back(second_taps, w_out)
    second_out, cotangent, text_embeds = ring.hold(second_out, cotangent, text_embeds)
    g_self.step()
    resnet = (masked + own_sum(second_out)) * keep
    resnet, cotangent, text_embeds = ring.hold(resnet, cotangent, text_embeds)
    g_self.step()

    attend_in, normal_self, scaling_self = norm_rows(resnet, gain_self_f)
    attend_all = flat(gather_rows(attend_in))
    g_text.begin()
    attend_all, cotangent = ring.hold(attend_all, cotangent)
    g_self.step()
    out_grad = cotangent.astype(f32) * keep
    feed_branch = flat(gather_rows(out_grad.astype(bf16)))
    w_self = g_self.whole
    qkv_full = w_self[:, : 3 * own_channels]
    cq_full = w_self[:, 3 * own_channels : 4 * own_channels]
    so_full = w_self[:, 4 * own_channels : 5 * own_channels]
    co_full = w_self[:, 5 * own_channels :]
    g_text.step()
    qkv = product(attend_all, qkv_full).astype(bf16)
    g_text.step()
    qkv = rows3(qkv)
    query_rows, key_rows, value_rows = jnp.split(qkv, 3, axis=2)
    mixture, self_chances = attend(query_rows, key_rows, value_rows, key_valid)
    self_part = product_back(flat(mixture), so_full)
    self_part = ring.hold(self_part)
    g_text.step()
    g_feed.begin()
    g_text.step()
    w_text = g_text.whole
    after_self = resnet + own_sum(self_part)
    g_feed.step()

    text_rows = flat(text_embeds)
    text_pair = product(text_rows, w_text).astype(bf16).reshape(slot_count, -1, 2 * own_channels)
    text_keys, text_values = jnp.split(text_pair, 2, axis=2)
    cross_in, normal_cross, scaling_cross = norm_rows(after_self, gain_cross_f)
    cross_all = flat(gather_rows(cross_in))
    cross_all = ring.hold(cross_all)
    g_feed.step()
    cross_rows = rows3(product(cross_all, cq_full).astype(bf16))
    cross_mix, cross_chances = attend(cross_rows, text_keys, text_values, None)
    cross_part = product_back(flat(cross_mix), co_full)
    cross_part = ring.hold(cross_part)
    g_feed.step()
    after_cross = after_self + own_sum(cross_part)

    feed_in, normal_feed, scaling_feed = norm_rows(after_cross, gain_feed_f)
    feed_in = ring.hold(feed_in)
    g_down.begin()
    g_feed.step()
    feed_all = flat(gather_rows(feed_in))
    w_feed = g_feed.whole
    g_down.step()
    pair_part = product(feed_all, w_feed)
    pair_part = ring.hold(pair_part)
    g_down.step()
    value_part, gate_part = pair_part[:, :hidden_own], pair_part[:, hidden_own:]
    lower = 0.5 * lax.erfc(-gate_part * math.sqrt(0.5))
    gelu_gate = gate_part * lower
    gelu_slope = lower + gate_part * jnp.exp(-0.5 * gate_part * gate_part) / math.sqrt(2 * math.pi)
    hidden = (value_part * gelu_gate).astype(bf16)
    hidden = ring.hold(hidden)
    g_down.step()
    s_down = Scattered(ring, weight_grad(feed_branch, hidden))
    g_down.step()
    w_down = g_down.whole

    s_down.step()
    hidden_grad = product(feed_branch, w_down)
    pair_grad = jnp.concatenate(
        [
            (hidden_grad * gelu_gate).astype(bf16),
            (hidden_grad * value_part * gelu_slope).astype(bf16),
        ],
        axis=1,
    )
    pair_grad = ring.hold(pair_grad)
    s_down.step()
    feed_part = product_back(pair_grad, w_feed)
    feed_part = ring.hold(feed_part)
    s_down.step()
    s_feed = Scattered(ring, weight_grad(feed_all, pair_grad))
    feed_back = own_sum(feed_part)
    feed_back = ring.hold(feed_back)
    s_down.step()
    feed_dv, grad_gain_feed = norm_rows_back(feed_back, normal_feed, scaling_feed, gain_feed_f)
    cross_grad = out_grad + feed_dv
    cross_branch = flat(gather_rows(cross_grad.astype(bf16)))
    cross_branch = ring.hold(cross_branch)
    s_feed.step()

    cross_mix_grad = rows3(product(cross_branch, co_full).astype(bf16))
    cross_dq, cross_dk, cross_dv = attend_back(
        cross_rows, text_keys, text_values, cross_mix_grad, cross_chances
    )
    cross_dq = flat(cross_dq)
    cross_dq, cross_dk, cross_dv = ring.hold(cross_dq, cross_dk, cross_dv)
    s_feed.step()
    cross_near = sum_near(product_back(cross_dq, cq_full), slot_count)
    cross_near = ring.hold(cross_near)
    s_feed.step()
    cross_back = sum_far(cross_near)
    grad_cross_out = weight_grad(cross_branch, flat(cross_mix))
    grad_cross_query = weight_grad(cross_all, cross_dq)
    s_cross = Scattered(
        ring,
        weight_grad(text_rows, flat(jnp.concatenate([cross_dk, cross_dv], axis=2))),
        jnp.concatenate([grad_cross_query, grad_cross_out], axis=1),
    )
    cross_dv_rows, grad_gain_cross = norm_rows_back(
        cross_back, normal_cross, scaling_cross, gain_cross_f
    )
    self_grad = cross_grad + cross_dv_rows

    self_branch = flat(gather_rows(self_grad.astype(bf16)))
    self_branch = ring.hold(self_branch)
    s_feed.step()
    mixture_grad = rows3(product(self_branch, so_full).astype(bf16))
    qkv_grad = flat(
        jnp.concatenate(
            attend_back(query_rows, key_rows, value_rows, mixture_grad, self_chances), axis=2
        )
    )
    qkv_grad = ring.hold(qkv_grad)
    s_cross.step()
    self_near = sum_near(product_back(qkv_grad, qkv_full), slot_count)
    self_near = ring.hold(self_near)
    s_cross.step()
    self_back = sum_far(self_near)
    self_dv_rows, grad_gain_self = norm_rows_back(self_back, normal_self, scaling_self, gain_self_f)
    resnet_grad = (self_grad + self_dv_rows) * keep
    resnet_branch = flat(gather_rows(resnet_grad.astype(bf16)))
    resnet_branch = ring.hold(resnet_branch)
    s_cross.step()

    second_parts = product(resnet_branch, w_out).astype(bf16)
    second_parts = ring.hold(second_parts)
    s_cross.step()
    grad_self_out = weight_grad(self_branch, flat(mixture))
    s_self = Scattered(
        ring, jnp.concatenate([weight_grad(attend_all, qkv_grad), grad_self_out], axis=1)
    )
    second_grad = shift_sum_back(tall, second_parts)
    second_grad = ring.hold(second_grad)
    s_self.step()
    s_out = Scattered(ring, weight_grad(resnet_branch, second_taps))
    mid_slope = silu_back(standard_mid * gain_mid_own, second_grad * keep_all)
    mid_gain_part = jnp.sum(mid_slope * standard_mid, axis=(0, 1))
    hat_mid = mid_slope * gain_mid_own
    mid_a = spread(group_sum(hat_mid, per_group) / counts[:, None], per_group)
    mid_b = spread(group_sum(hat_mid * standard_mid, per_group) / counts[:, None], per_group)
    middle_grad = (
        scaling_mid * (hat_mid - (mid_a + standard_mid * mid_b)) * keep_all
    ).astype(bf16)
    middle_grad = ring.hold(middle_grad)
    s_self.step()
    middle_taps = shift_stack_back(wide, flat(middle_grad))
    middle_taps = ring.hold(middle_taps)
    s_self.step()
    first_near = sum_near(product_back(middle_taps, w_in), slot_count)
    first_near = ring.hold(first_near)
    s_self.step()
    in_grad = weight_grad(first_all, middle_taps)
    cut = in_grad.shape[1] // 256 * 128
    s_in = Scattered(ring, in_grad[:, :cut])
    first_grad = sum_far(first_near)
    first_grad, hidden, middle_grad = ring.hold(first_grad, hidden, middle_grad)
    s_out.step()

    in_slope = silu_back(standard_in * gain_in_f, first_grad * keep)
    in_gain_part = jnp.sum(in_slope * standard_in, axis=(0, 1))
    hat_in = in_slope * gain_in_f
    in_a, in_b = lax.psum(
        (group_sum(hat_in, per_group), group_sum(hat_in * standard_in, per_group)), "mp"
    )
    in_a, in_b, in_gain_part, middle_grad, hidden = ring.hold(
        in_a, in_b, in_gain_part, middle_grad, hidden
    )
    s_out.step()
    in_a = spread(in_a / counts[:, None], per_group)
    in_b = spread(in_b / counts[:, None], per_group)
    grouped_grad = scaling_in * (hat_in - (in_a + standard_in * in_b))
    latent_grad = ((resnet_grad + grouped_grad) * keep).astype(bf16)

    latent_grad, in_gain_part, middle_grad, hidden = ring.hold(
        latent_grad, in_gain_part, middle_grad, hidden
    )
    s_out.step()
    s_out.step()
    in_gain_part, middle_grad, hidden = ring.hold(in_gain_part, middle_grad, hidden)
    other = Ring()
    other.last = ring.last
    s_rest = Scattered(other, in_grad[:, cut:])
    s_in.step()
    s_rest.step()

    mid_gain_whole = lax.dynamic_update_slice_in_dim(
        jnp.zeros((channels,), f32), mid_gain_part, channel_start, 0
    )
    gain_parts = jnp.stack(
        [in_gain_part, mid_gain_whole, grad_gain_self, grad_gain_cross, grad_gain_feed]
    )
    gain_parts = jnp.swapaxes(gain_parts.reshape(5, dp_size, share), 0, 1)
    gain_parts = jnp.broadcast_to(gain_parts[:, None], (dp_size, mp_size, 5, share))
    time_sum = jnp.sum(middle_grad.astype(f32), axis=1).reshape(1, -1)
    payload = jnp.concatenate(
        [
            gain_parts.reshape(dp_size * mp_size, 5 * share),
            jnp.broadcast_to(time_sum, (dp_size * mp_size, time_sum.shape[1])),
        ],
        axis=1,
    )
    payload = lax.all_to_all(payload, ("dp", "mp"), 0, 0, tiled=True)
    gain_sums = payload[:, : 5 * share].sum(0).reshape(5, share)
    time_sum_all = payload[:, 5 * share :].reshape(dp_size, mp_size, -1)
    time_sum_all = lax.dynamic_index_in_dim(time_sum_all, mp_index, 1, keepdims=False)
    grad_time = jnp.einsum(
        "sa,sb->ab",
        time_act.astype(f32),
        time_sum_all.reshape(-1, own_channels),
        precision=highest,
        preferred_element_type=f32,
    )
    gain_sums, grad_time, hidden = ring.hold(gain_sums, grad_time, hidden)
    s_in.step()
    s_rest.step()
    output_near = sum_near(product_back(hidden, w_down), slot_count)
    s_in.step()
    s_rest.step()
    output = ((after_cross + sum_far(output_near)) * keep).astype(bf16)
    s_in.step()
    s_rest.step()
    sum_in = jnp.concatenate([s_in.part, s_rest.part], axis=1)
    sum_out, sum_self = s_out.part, s_self.part
    sum_feed, sum_down = s_feed.part, s_down.part
    text_share = cross_key.shape[0]
    sum_text, sum_cross = s_cross.part[:text_share], s_cross.part[text_share:]

    def tap_part(values, tap):
        return values[:, tap * own_channels : (tap + 1) * own_channels]

    def column_part(values, part):
        return values[:, part * own_channels : (part + 1) * own_channels]

    return (
        output,
        latent_grad,
        jnp.stack([tap_part(sum_in, t) for t in range(TAPS)]).reshape(conv_in.shape),
        jnp.stack([tap_part(sum_out, t).T for t in range(TAPS)]).reshape(conv_out.shape),
        grad_time,
        column_part(sum_self, 0),
        column_part(sum_self, 1),
        column_part(sum_self, 2),
        column_part(sum_self, 3).T,
        column_part(sum_cross, 0),
        column_part(sum_text, 0),
        column_part(sum_text, 1),
        column_part(sum_cross, 1).T,
        sum_feed[:, :hidden_own],
        sum_feed[:, hidden_own:],
        sum_down.T,
        gain_sums[0],
        gain_sums[1],
        gain_sums[2],
        gain_sums[3],
        gain_sums[4],
    )


def solution(mesh):
    in_specs = (
        P("dp", "mp", None),
        P("dp", None, None),
        P("dp", "mp", None),
        P("dp"),
        P("dp"),
        P("dp"),
        P(None, None, "dp", "mp"),
        P(None, None, "mp", "dp"),
        P("dp", "mp"),
        P("dp", "mp"),
        P("dp", "mp"),
        P("dp", "mp"),
        P("mp", "dp"),
        P("dp", "mp"),
        P("dp", "mp"),
        P("dp", "mp"),
        P("mp", "dp"),
        P("dp", "mp"),
        P("dp", "mp"),
        P("mp", "dp"),
        P("dp"),
        P("dp"),
        P("dp"),
        P("dp"),
        P("dp"),
    )
    out_specs = (
        P("dp", "mp", None),
        P("dp", "mp", None),
        P(None, None, "dp", "mp"),
        P(None, None, "mp", "dp"),
        P("dp", "mp"),
        P("dp", "mp"),
        P("dp", "mp"),
        P("dp", "mp"),
        P("mp", "dp"),
        P("dp", "mp"),
        P("dp", "mp"),
        P("dp", "mp"),
        P("mp", "dp"),
        P("dp", "mp"),
        P("dp", "mp"),
        P("mp", "dp"),
        P("dp"),
        P("dp"),
        P("dp"),
        P("dp"),
        P("dp"),
    )
    return jax.shard_map(body, mesh=mesh, in_specs=in_specs, out_specs=out_specs, check_vma=False)
```
